32 devices in a mesh: groups: 2 (over y), tm: 4 (over x, core), win: 4 (over z).
Axes of the slice: x: 2, y: 2, z: 4, core: 2. Of those that a mesh axis runs over, the one named last changes fastest.
Arguments:
- unitaries: float32 [8, 4, 2, 2, 256, 256], P(('groups', 'win'), 'tm'), parts along dimension 0, may hold values from -1 to 1, as said below
Outputs:
- propagators: float32 [8, 4, 2, 2, 256, 256], P(('groups', 'win'), 'tm'), parts along dimension 0
The draws below stay inside these ranges and needn't reach their ends.
There are 2 independent parts, one for each index of `groups`. The reference program is written for one: setup_inputs(seed, part) draws one part's arguments, and reference() takes and returns one part's arrays. A program takes and returns all parts, laid end to end along the dimension named above; each array names one. Nothing has to cross between parts.
Inputs may be any that keep to these rules, and one draw needn't show every extreme that they name: `unitaries`: each slot's complex matrix is unitary.
All inputs are finite; a program needn't handle non-finite values.
Results may differ from the reference program's by a relative error of at most 0.0003.
Values sent between devices are 32-bit elements; how exact they have to be, the bound alone decides.
No kernel may reach another device: no remote copies, remote signals or barrier semaphores. Data moves between devices by JAX's collectives and lax.ppermute only.
A program may use at most 64 MiB of HBM per device.

```python
import math
import jax
import jax.numpy as jnp
from jax import lax

DIM = 256
SLOTS = 2
WIN_DEVS = 4
WINDOWS = 4


def draw_unitaries(key, part):
    slot_count = WINDOWS * WIN_DEVS * SLOTS
    qubits = DIM.bit_length() - 1
    subkeys = jax.random.split(key, 3)

    def rotations(rkey):
        akey, bkey, ckey = jax.random.split(rkey, 3)
        tilt_angle = jax.random.uniform(akey, (slot_count, qubits), jnp.float32, 0.25, 1.3)
        phase_one = jax.random.uniform(bkey, (slot_count, qubits), jnp.float32, -math.pi, math.pi)
        phase_two = jax.random.uniform(ckey, (slot_count, qubits), jnp.float32, -math.pi, math.pi)
        cosine = jnp.cos(tilt_angle)
        sine = jnp.sin(tilt_angle)
        top_real = jnp.stack([cosine * jnp.cos(phase_one), -sine * jnp.cos(phase_two)], axis=-1)
        low_real = jnp.stack([sine * jnp.cos(phase_two), cosine * jnp.cos(phase_one)], axis=-1)
        top_imag = jnp.stack([cosine * jnp.sin(phase_one), sine * jnp.sin(phase_two)], axis=-1)
        low_imag = jnp.stack([sine * jnp.sin(phase_two), -cosine * jnp.sin(phase_one)], axis=-1)
        return (jnp.stack([top_real, low_real], axis=-2), jnp.stack([top_imag, low_imag], axis=-2))
    first_real, first_imag = rotations(subkeys[0])
    kron_real = jnp.ones((slot_count, 1, 1), jnp.float32)
    kron_imag = jnp.zeros((slot_count, 1, 1), jnp.float32)
    for q in range(qubits):
        gate_real = first_real[:, q]
        gate_imag = first_imag[:, q]
        size_now = kron_real.shape[1] * 2
        new_real = kron_real[:, :, None, :, None] * gate_real[:, None, :, None, :] - kron_imag[:, :, None, :, None] * gate_imag[:, None, :, None, :]
        new_imag = kron_real[:, :, None, :, None] * gate_imag[:, None, :, None, :] + kron_imag[:, :, None, :, None] * gate_real[:, None, :, None, :]
        kron_real = new_real.reshape((slot_count, size_now, size_now))
        kron_imag = new_imag.reshape((slot_count, size_now, size_now))
    phases = jax.random.uniform(subkeys[1], (slot_count, DIM, 1), jnp.float32, -math.pi, math.pi)
    mixed_real = jnp.cos(phases) * kron_real - jnp.sin(phases) * kron_imag
    mixed_imag = jnp.cos(phases) * kron_imag + jnp.sin(phases) * kron_real
    second_real, second_imag = rotations(subkeys[2])
    for q in range(qubits):
        gate_real = second_real[:, q]
        gate_imag = second_imag[:, q]
        shaped = (slot_count, 2 ** q, 2, 2 ** (qubits - 1 - q), DIM)
        block_real = mixed_real.reshape(shaped)
        block_imag = mixed_imag.reshape(shaped)
        new_real = jnp.einsum('nij,najbc->naibc', gate_real, block_real) - jnp.einsum('nij,najbc->naibc', gate_imag, block_imag)
        new_imag = jnp.einsum('nij,najbc->naibc', gate_real, block_imag) + jnp.einsum('nij,najbc->naibc', gate_imag, block_real)
        mixed_real = new_real.reshape((slot_count, DIM, DIM))
        mixed_imag = new_imag.reshape((slot_count, DIM, DIM))
    stacked = jnp.stack([mixed_real, mixed_imag], axis=1)
    return stacked.reshape((WINDOWS, WIN_DEVS, SLOTS, 2, DIM, DIM)).astype(jnp.float32)


def setup_inputs(seed: int = 0, part: int = 0) -> dict:
    arg_keys = jax.random.split(jax.random.key(seed), 2)
    part_splits = jax.random.split(jax.random.fold_in(arg_keys[1], part), 2)
    unitaries = draw_unitaries(jax.random.fold_in(jax.random.fold_in(arg_keys[1], part), 71), part)
    return {"unitaries": unitaries}


def complex_product(left, right):
    hi = lax.Precision.HIGHEST
    real_part = jnp.dot(left[0], right[0], precision=hi, preferred_element_type=jnp.float32) - jnp.dot(left[1], right[1], precision=hi, preferred_element_type=jnp.float32)
    imag_part = jnp.dot(left[0], right[1], precision=hi, preferred_element_type=jnp.float32) + jnp.dot(left[1], right[0], precision=hi, preferred_element_type=jnp.float32)
    return jnp.stack([real_part, imag_part])


def reference(unitaries):
    shape = unitaries.shape
    width = shape[-1]
    sequence = unitaries.reshape((-1, 2, width, width))
    start = jnp.stack([jnp.eye(width, dtype=jnp.float32), jnp.zeros((width, width), jnp.float32)])

    def advance(running, factor):
        updated = complex_product(factor, running)
        return updated, updated

    final_value, history = lax.scan(advance, start, sequence)
    return history.reshape(shape)
```

```python
import functools

import jax
import jax.numpy as jnp
from jax import lax
from jax.experimental import pallas as pl
from jax.experimental.pallas import tpu as pltpu
from jax.sharding import PartitionSpec as P

F32 = jnp.float32
AXES = ("tm", "win")
NN = (((1,), (0,)), ((), ()))
NT = (((1,), (1,)), ((), ()))


def halves(x):
    high = x.astype(jnp.bfloat16)
    return high, (x - high.astype(F32)).astype(jnp.bfloat16)


def product(left, right, dims=NN):
    (lr, lrl), (li, lil) = halves(left[0]), halves(left[1])
    (rr, rrl), (ri, ril) = halves(right[0]), halves(right[1])
    dot = functools.partial(
        lax.dot_general, dimension_numbers=dims, preferred_element_type=F32
    )

    def real(a, al, b, bl):
        return dot(a, b) + (dot(a, bl) + dot(al, b))

    return (
        real(lr, lrl, rr, rrl) - real(li, lil, ri, ril),
        real(lr, lrl, ri, ril) + real(li, lil, rr, rrl),
    )


def pick(condition, yes, no):
    return tuple(jnp.where(condition, a, b) for a, b in zip(yes, no, strict=True))


def pair(ref):
    return ref[0], ref[1]


def put(ref, value):
    ref[0] = value[0]
    ref[1] = value[1]


def identity(width):
    rows = lax.broadcasted_iota(jnp.int32, (width, width), 0)
    columns = lax.broadcasted_iota(jnp.int32, (width, width), 1)
    one = (rows == columns).astype(F32)
    return one, jnp.zeros_like(one)


def call(body, outs, *operands, name):
    whole = pl.BlockSpec(memory_space=pltpu.VMEM)
    shapes = [jax.ShapeDtypeStruct(shape, F32) for shape in outs]
    return pl.pallas_call(
        body,
        out_shape=shapes,
        in_specs=[whole] * len(operands),
        out_specs=[whole] * len(outs),
        compiler_params=pltpu.CompilerParams(vmem_limit_bytes=32 << 20),
        name=name,
    )(*operands)


def place():
    t, w = lax.axis_index("tm"), lax.axis_index("win")
    return t // 2, t % 2, w


def block_kernel(u, block, turned):
    b = product(pair(u[0, 0, 1]), pair(u[0, 0, 0]))
    put(block, b)
    put(turned, (b[0].T, b[1].T))


def chip_kernel(mine, theirs, chip, plane):
    _, k, _ = place()
    first = pick(k == 0, pair(mine), pair(theirs))
    second = pick(k == 0, pair(theirs), pair(mine))
    value = product(first, second)
    put(chip, value)
    plane[...] = jnp.where(k == 0, value[0], value[1])


def window_kernel(chip, near, far, window, piece):
    x, k, _ = place()
    mine = pair(chip)
    other = pick(k == 0, (near[...], far[...]), (far[...], near[...]))
    value = product(pick(x == 0, mine, other), pick(x == 0, other, mine))
    put(window, value)
    rows = piece.shape[1]
    start = pl.multiple_of((2 * k + x) * rows, rows)
    piece[...] = window[:, pl.ds(start, rows), :]


def extend_kernel(piece, window, out):
    put(out, product(pair(piece), pair(window)))


def join(flag, a, b):
    return tuple(
        jnp.concatenate([jnp.where(flag, p, q), jnp.where(flag, q, p)], axis=0)
        for p, q in zip(a, b, strict=True)
    )


def left_kernel(u, block, turned, near_chip, far_chip, near, far, out):
    x, k, w = place()
    width = block.shape[-1]
    one = identity(width)
    other_chip = pick(k == 0, (near_chip[...], far_chip[...]), (far_chip[...], near_chip[...]))
    earlier = product(pick(x == 1, other_chip, one), pick(k == 1, pair(turned), one))
    mine = join(x == 0, pair(near[0]), pair(near[1]))
    theirs = join(x == 0, pair(far[0]), pair(far[1]))
    window = pick(w >= 2, join(k == 0, mine, theirs), one)
    before = product(window, earlier)
    put(out.at[0], product(pair(u[0, 0, 0]), before, NT))
    put(out.at[1], product(pair(block), before, NT))


def final_kernel(left, near, far, out):
    x, k, w = place()
    mine = join(x == 0, pair(near[0]), pair(near[1]))
    theirs = join(x == 0, pair(far[0]), pair(far[1]))
    offset = pick(w >= 1, join(k == 0, mine, theirs), identity(left.shape[-1]))
    for slot in range(2):
        put(out.at[0, 0, slot], product(pair(left[slot]), offset, NT))


def permute(value, pairs):
    windows = lax.axis_size("win")
    flat = [(a * windows + b, c * windows + d) for (a, b), (c, d) in pairs]
    return lax.ppermute(value, AXES, flat)


def small(unitaries):
    width = unitaries.shape[-1]
    full, rows = (2, width, width), width // 4
    strip = (2, rows, width)
    tms, wins = range(4), range(4)
    w = lax.axis_index("win")
    cores = [((t, v), (t ^ 1, v)) for t in tms for v in wins]

    block, turned = call(block_kernel, [full, full], unitaries, name="block")
    turned_other = permute(turned, cores)
    chip, plane = call(chip_kernel, [full, full[1:]], turned, turned_other, name="chip")
    near_chip = permute(plane, [((t, v), (t ^ 2, v)) for t in tms for v in wins])
    far_chip = permute(near_chip, cores)
    window, piece = call(window_kernel, [full, strip], chip, near_chip, far_chip, name="window")

    one_on = permute(piece, [((t, v), (t, v + 1)) for t in tms for v in wins[:-1]])
    two_on = permute(piece, [((t, 0), (t, 2)) for t in tms])
    (both,) = call(extend_kernel, [strip], one_on, window, name="extend")
    both_on = permute(both, [((t, 1), (t, 3)) for t in tms])
    one_across = permute(one_on, [((t, v), (t ^ 2, v)) for t in tms for v in wins[1:]])
    across = permute(
        jnp.where(w == 2, two_on, both),
        [((t, 1), (t ^ 2, 3)) for t in tms] + [((t, 2), (t ^ 2, 2)) for t in tms],
    )

    near_one = jnp.stack([one_on, one_across])
    far_one = permute(near_one, cores)
    (left,) = call(
        left_kernel, [(2, *full)], unitaries, block, turned_other, near_chip, far_chip, near_one, far_one, name="left"
    )

    near = jnp.where(
        w == 1,
        near_one,
        jnp.stack([jnp.where(w == 2, two_on, both_on), across]),
    )
    far = permute(near, cores)
    (out,) = call(final_kernel, [unitaries.shape], left, near, far, name="final")
    return out


def multiply(left, right):
    def body(a, b, out):
        put(out, product(pair(a), pair(b)))

    return call(body, [right.shape], left, right, name="multiply")[0]


def scan(value, axis):
    count, mine = lax.axis_size(axis), lax.axis_index(axis)
    width = value.shape[-1]
    one = jnp.stack([jnp.eye(width, dtype=F32), jnp.zeros((width, width), F32)])
    shifted = lax.ppermute(value, axis, [(i, i + 1) for i in range(count - 1)])
    running = jnp.where(mine >= 1, shifted, one)
    step = 1
    while step < count - 1:
        arrived = lax.ppermute(running, axis, [(i, i + step) for i in range(count - step)])
        running = multiply(running, jnp.where(mine >= step, arrived, one))
        step *= 2
    return running


def general(unitaries):
    own = unitaries[0, 0]
    count = lax.axis_size("tm")
    block = multiply(own[1], own[0])
    before = scan(block, "tm")
    through = multiply(block, before)
    step, mine = 1, lax.axis_index("tm")
    total = through
    while step < count:
        pairs = [(count - 1 - i, count - 1 - i - step) for i in range(min(step, count - step))]
        arrived = lax.ppermute(total, "tm", pairs)
        behind = count - 1 - mine
        total = jnp.where((behind >= step) & (behind < 2 * step), arrived, total)
        step *= 2
    offset = multiply(before, scan(total, "win"))
    first = multiply(own[0], offset)
    return jnp.stack([first, multiply(own[1], first)])[None, None]


def solution(mesh):
    spec = P(("groups", "win"), "tm", None, None, None, None)
    plain = mesh.shape["tm"] == 4 and mesh.shape["win"] == 4
    return jax.shard_map(
        small if plain else general,
        mesh=mesh,
        in_specs=(spec,),
        out_specs=spec,
        check_vma=False,
    )
```

```python
import functools

import jax
import jax.numpy as jnp
from jax import lax
from jax.experimental import pallas as pl
from jax.experimental.pallas import tpu as pltpu
from jax.sharding import PartitionSpec as P

F32 = jnp.float32
AXES = ("tm", "win")
NN = (((1,), (0,)), ((), ()))
NT = (((1,), (1,)), ((), ()))


def halves(x):
    high = x.astype(jnp.bfloat16)
    return high, (x - high.astype(F32)).astype(jnp.bfloat16)


def product(left, right, dims=NN):
    (lr, lrl), (li, lil) = halves(left[0]), halves(left[1])
    (rr, rrl), (ri, ril) = halves(right[0]), halves(right[1])
    dot = functools.partial(
        lax.dot_general, dimension_numbers=dims, preferred_element_type=F32
    )

    def real(a, al, b, bl):
        return dot(a, b) + (dot(a, bl) + dot(al, b))

    return (
        real(lr, lrl, rr, rrl) - real(li, lil, ri, ril),
        real(lr, lrl, ri, ril) + real(li, lil, rr, rrl),
    )


def pick(condition, yes, no):
    return tuple(jnp.where(condition, a, b) for a, b in zip(yes, no, strict=True))


def pair(ref):
    return ref[0], ref[1]


def put(ref, value):
    ref[0] = value[0]
    ref[1] = value[1]


def identity(width):
    rows = lax.broadcasted_iota(jnp.int32, (width, width), 0)
    columns = lax.broadcasted_iota(jnp.int32, (width, width), 1)
    one = (rows == columns).astype(F32)
    return one, jnp.zeros_like(one)


def call(body, outs, *operands, name, scratch=()):
    whole = pl.BlockSpec(memory_space=pltpu.VMEM)
    shapes = [jax.ShapeDtypeStruct(shape, F32) for shape in outs]
    return pl.pallas_call(
        body,
        out_shape=shapes,
        in_specs=[whole] * len(operands),
        out_specs=[whole] * len(outs),
        scratch_shapes=[pltpu.VMEM(shape, F32) for shape in scratch],
        compiler_params=pltpu.CompilerParams(vmem_limit_bytes=32 << 20),
        name=name,
    )(*operands)


def place():
    t, w = lax.axis_index("tm"), lax.axis_index("win")
    return t // 2, t % 2, w


def block_kernel(u, block, turned):
    b = product(pair(u[0, 0, 1]), pair(u[0, 0, 0]))
    put(block, b)
    put(turned, (b[0].T, b[1].T))


def chip_kernel(mine, theirs, chip, plane):
    _, k, _ = place()
    first = pick(k == 0, pair(mine), pair(theirs))
    second = pick(k == 0, pair(theirs), pair(mine))
    value = product(first, second)
    put(chip, value)
    plane[...] = jnp.where(k == 0, value[0], value[1])


def ordered(x, k, chip, near, far):
    mine = pair(chip)
    other = pick(k == 0, (near[...], far[...]), (far[...], near[...]))
    return pick(x == 0, mine, other), pick(x == 0, other, mine)


def window_kernel(chip, near, far, window, own, other):
    x, k, _ = place()
    put(window, product(*ordered(x, k, chip, near, far)))
    rows = own.shape[1]
    for strip, at in ((own, x), (other, 1 - x)):
        strip[...] = window[:, pl.ds(pl.multiple_of((2 * k + at) * rows, rows), rows), :]


def extend_kernel(piece, window, out):
    put(out, product(pair(piece), pair(window)))


def stack(upper, lower):
    return tuple(jnp.concatenate([a, b], axis=0) for a, b in zip(upper, lower, strict=True))


def whole(near, across, far, far_across):
    x, k, _ = place()
    near, across, far, far_across = map(pair, (near, across, far, far_across))
    mine = stack(pick(x == 0, near, across), pick(x == 0, across, near))
    theirs = stack(pick(x == 0, far, far_across), pick(x == 0, far_across, far))
    return stack(pick(k == 0, mine, theirs), pick(k == 0, theirs, mine))


def before_kernel(u, block, turned, near, far, out):
    x, k, _ = place()
    one = identity(block.shape[-1])
    other = pick(k == 0, (near[...], far[...]), (far[...], near[...]))
    before = product(pick(x == 1, other, one), pick(k == 1, pair(turned), one))
    put(out.at[0], product(pair(u[0, 0, 0]), before, NT))
    put(out.at[1], product(pair(block), before, NT))


def left_kernel(before, near, across, far, far_across, out):
    _, _, w = place()
    window = pick(w == 3, whole(near, across, far, far_across), identity(before.shape[-1]))
    for slot in range(2):
        put(out.at[slot], product(pair(before[slot]), window, NT))


def merge_kernel(one, two, three, out):
    _, _, w = place()
    out[...] = jnp.where(w == 1, one[...], jnp.where(w == 2, two[...], three[...]))


def final_kernel(left, near, across, far, far_across, out):
    _, _, w = place()
    offset = pick(w >= 1, whole(near, across, far, far_across), identity(left.shape[-1]))
    for slot in range(2):
        put(out.at[0, 0, slot], product(pair(left[slot]), offset, NT))


def permute(value, pairs):
    windows = lax.axis_size("win")
    flat = [(a * windows + b, c * windows + d) for (a, b), (c, d) in pairs]
    return lax.ppermute(value, AXES, flat)


def small(unitaries):
    width = unitaries.shape[-1]
    full, strip = (2, width, width), (2, width // 4, width)
    spots = [(t, v) for t in range(4) for v in range(4)]
    cores = [((t, v), (t ^ 1, v)) for t, v in spots]
    chips = [((t, v), (t ^ 2, v)) for t, v in spots]
    twins = [((t, v), (t, v ^ 1)) for t, v in spots]
    one_two = [((t, 1), (t, 2)) for t in range(4)]
    one_three = [((t, 1), (t, 3)) for t in range(4)]
    tie = lax.optimization_barrier

    block, turned = call(block_kernel, [full, full], unitaries, name="block")
    turned_other = permute(turned, cores)
    chip, plane = call(chip_kernel, [full, full[1:]], turned, turned_other, name="chip")
    near_chip = permute(plane, chips)
    far_chip = permute(near_chip, cores)
    window, own, other = call(window_kernel, [full, strip, strip], chip, near_chip, far_chip, name="window")

    one, one_other = permute(own, twins), permute(other, twins)
    (before,) = call(
        before_kernel, [(2, *full)], unitaries, block, turned_other, near_chip, far_chip, name="before"
    )
    one, before = tie((one, before))
    (both,) = call(extend_kernel, [strip], one, window, name="extend")
    two = permute(both, one_two)
    (both_other,) = call(extend_kernel, [strip], one_other, window, name="extend_other")
    three_other = permute(both_other, one_three)
    three = permute(two, twins)
    two_other = permute(two, chips)

    (across,) = call(merge_kernel, [strip], one_other, two_other, three_other, name="merge_across")
    far_across = permute(across, cores)
    three, across = tie((three, across))
    (near,) = call(merge_kernel, [strip], one, two, three, name="merge_near")
    far = permute(near, cores)
    one, one_other, _ = tie((one, one_other, both_other))
    (left,) = call(
        left_kernel, [(2, *full)], before, one, one_other, permute(one, cores), permute(one_other, cores), name="left"
    )
    (out,) = call(final_kernel, [unitaries.shape], left, near, across, far, far_across, name="final")
    return out


def multiply(left, right):
    def body(a, b, out):
        put(out, product(pair(a), pair(b)))

    return call(body, [right.shape], left, right, name="multiply")[0]


def scan(value, axis):
    count, mine = lax.axis_size(axis), lax.axis_index(axis)
    width = value.shape[-1]
    one = jnp.stack([jnp.eye(width, dtype=F32), jnp.zeros((width, width), F32)])
    shifted = lax.ppermute(value, axis, [(i, i + 1) for i in range(count - 1)])
    running = jnp.where(mine >= 1, shifted, one)
    step = 1
    while step < count - 1:
        arrived = lax.ppermute(running, axis, [(i, i + step) for i in range(count - step)])
        running = multiply(running, jnp.where(mine >= step, arrived, one))
        step *= 2
    return running


def general(unitaries):
    own = unitaries[0, 0]
    count = lax.axis_size("tm")
    block = multiply(own[1], own[0])
    before = scan(block, "tm")
    through = multiply(block, before)
    step, mine = 1, lax.axis_index("tm")
    total = through
    while step < count:
        pairs = [(count - 1 - i, count - 1 - i - step) for i in range(min(step, count - step))]
        arrived = lax.ppermute(total, "tm", pairs)
        behind = count - 1 - mine
        total = jnp.where((behind >= step) & (behind < 2 * step), arrived, total)
        step *= 2
    offset = multiply(before, scan(total, "win"))
    first = multiply(own[0], offset)
    return jnp.stack([first, multiply(own[1], first)])[None, None]


def solution(mesh):
    spec = P(("groups", "win"), "tm", None, None, None, None)
    plain = mesh.shape["tm"] == 4 and mesh.shape["win"] == 4
    return jax.shard_map(
        small if plain else general,
        mesh=mesh,
        in_specs=(spec,),
        out_specs=spec,
        check_vma=False,
    )
```

```python
import functools

import jax
import jax.numpy as jnp
from jax import lax
from jax.experimental import pallas as pl
from jax.experimental.pallas import tpu as pltpu
from jax.sharding import PartitionSpec as P

F32 = jnp.float32
AXES = ("tm", "win")
NN = (((1,), (0,)), ((), ()))
NT = (((1,), (1,)), ((), ()))


def halves(x):
    high = x.astype(jnp.bfloat16)
    return high, (x - high.astype(F32)).astype(jnp.bfloat16)


def product(left, right, dims=NN):
    (lr, lrl), (li, lil) = halves(left[0]), halves(left[1])
    (rr, rrl), (ri, ril) = halves(right[0]), halves(right[1])
    dot = functools.partial(
        lax.dot_general, dimension_numbers=dims, preferred_element_type=F32
    )

    def real(a, al, b, bl):
        return dot(a, b) + (dot(a, bl) + dot(al, b))

    return (
        real(lr, lrl, rr, rrl) - real(li, lil, ri, ril),
        real(lr, lrl, ri, ril) + real(li, lil, rr, rrl),
    )


def pick(condition, yes, no):
    return tuple(jnp.where(condition, a, b) for a, b in zip(yes, no, strict=True))


def pair(ref):
    return ref[0], ref[1]


def put(ref, value):
    ref[0] = value[0]
    ref[1] = value[1]


def identity(width):
    rows = lax.broadcasted_iota(jnp.int32, (width, width), 0)
    columns = lax.broadcasted_iota(jnp.int32, (width, width), 1)
    one = (rows == columns).astype(F32)
    return one, jnp.zeros_like(one)


def call(body, outs, *operands, name, scratch=(), hbm_out=False, alias=None):
    whole, far = pl.BlockSpec(memory_space=pltpu.VMEM), pl.BlockSpec(memory_space=pl.ANY)
    shapes = [jax.ShapeDtypeStruct(shape, F32) for shape in outs]
    return pl.pallas_call(
        body,
        out_shape=shapes,
        in_specs=[far if i == alias else whole for i in range(len(operands))],
        out_specs=[far if hbm_out else whole] * len(outs),
        input_output_aliases={} if alias is None else {alias: 0},
        scratch_shapes=list(scratch),
        compiler_params=pltpu.CompilerParams(vmem_limit_bytes=32 << 20),
        name=name,
    )(*operands)


def place():
    t, w = lax.axis_index("tm"), lax.axis_index("win")
    return t // 2, t % 2, w


def block_kernel(u, block, turned):
    b = product(pair(u[0, 0, 1]), pair(u[0, 0, 0]))
    put(block, b)
    put(turned, (b[0].T, b[1].T))


def chip_kernel(mine, theirs, chip, plane):
    _, k, _ = place()
    first = pick(k == 0, pair(mine), pair(theirs))
    second = pick(k == 0, pair(theirs), pair(mine))
    value = product(first, second)
    put(chip, value)
    plane[...] = jnp.where(k == 0, value[0], value[1])


def ordered(x, k, chip, near, far):
    mine = pair(chip)
    other = pick(k == 0, (near[...], far[...]), (far[...], near[...]))
    return pick(x == 0, mine, other), pick(x == 0, other, mine)


def window_kernel(chip, near, far, window, own, other):
    x, k, _ = place()
    put(window, product(*ordered(x, k, chip, near, far)))
    rows = own.shape[1]
    for strip, at in ((own, x), (other, 1 - x)):
        strip[...] = window[:, pl.ds(pl.multiple_of((2 * k + at) * rows, rows), rows), :]


def extend_kernel(piece, window, out):
    _, _, w = place()

    @pl.when(w == 1)
    def _():
        put(out, product(pair(piece), pair(window)))


def stack(upper, lower):
    return tuple(jnp.concatenate([a, b], axis=0) for a, b in zip(upper, lower, strict=True))


def half(x, near, across):
    near, across = pair(near), pair(across)
    return stack(pick(x == 0, near, across), pick(x == 0, across, near))


def whole(near, across, far, far_across):
    x, k, _ = place()
    mine, theirs = half(x, near, across), half(x, far, far_across)
    return stack(pick(k == 0, mine, theirs), pick(k == 0, theirs, mine))


def before_kernel(u, block, turned, near, far, out):
    x, k, _ = place()
    one = identity(block.shape[-1])
    other = pick(k == 0, (near[...], far[...]), (far[...], near[...]))
    before = product(pick(x == 1, other, one), pick(k == 1, pair(turned), one))
    put(out.at[0], product(pair(u[0, 0, 0]), before, NT))
    put(out.at[1], product(pair(block), before, NT))


def left_kernel(before, near, across, far, far_across, out):
    _, _, w = place()

    @pl.when(w == 3)
    def _():
        window = whole(near, across, far, far_across)
        for slot in range(2):
            put(out.at[slot], product(pair(before[slot]), window, NT))

    @pl.when(w != 3)
    def _():
        out[...] = before[...]


def merge_kernel(one, two, three, out):
    _, _, w = place()
    out[...] = jnp.where(w == 1, one[...], jnp.where(w == 2, two[...], three[...]))


def send(out, columns, at, sems, left, offset):
    width, copies = columns.shape[-1], []
    high, low = halves(jnp.concatenate(offset, axis=0))
    dot = functools.partial(lax.dot_general, dimension_numbers=NT, preferred_element_type=F32)
    for slot in range(2):
        parts = []
        for plane in range(2):
            a, al = halves(left[slot, plane])
            parts.append(dot(a, high) + (dot(a, low) + dot(al, high)))
        real, imag = parts
        columns[slot, 0] = real[:, :width] - imag[:, width:]
        columns[slot, 1] = real[:, width:] + imag[:, :width]
        copies.append(pltpu.make_async_copy(columns.at[slot], out.at[0, 0, slot, :, :, at], sems.at[slot]))
        copies[-1].start()
    return copies


def near_kernel(left, near, across, out, columns, sems):
    x, k, w = place()
    width = columns.shape[-1]

    @pl.when(w == 0)
    def _():
        copies = [pltpu.make_async_copy(left.at[s], out.at[0, 0, s], sems.at[s]) for s in range(2)]
        for copy in copies:
            copy.start()
        for copy in copies:
            copy.wait()

    @pl.when(w != 0)
    def _():
        at = pl.ds(pl.multiple_of(k * width, width), width)
        for copy in send(out, columns, at, sems, left, half(x, near, across)):
            copy.wait()


def far_kernel(_, left, far, far_across, out, columns, sems):
    x, k, w = place()
    width = columns.shape[-1]

    @pl.when(w != 0)
    def _():
        at = pl.ds(pl.multiple_of((1 - k) * width, width), width)
        for copy in send(out, columns, at, sems, left, half(x, far, far_across)):
            copy.wait()


def permute(value, pairs):
    windows = lax.axis_size("win")
    flat = [(a * windows + b, c * windows + d) for (a, b), (c, d) in pairs]
    return lax.ppermute(value, AXES, flat)


def small(unitaries):
    width = unitaries.shape[-1]
    full, strip = (2, width, width), (2, width // 4, width)
    spots = [(t, v) for t in range(4) for v in range(4)]
    cores = [((t, v), (t ^ 1, v)) for t, v in spots]
    chips = [((t, v), (t ^ 2, v)) for t, v in spots]
    twins = [((t, v), (t, v ^ 1)) for t, v in spots]
    one_two = [((t, 1), (t, 2)) for t in range(4)]
    one_three = [((t, 1), (t, 3)) for t in range(4)]
    tie = lax.optimization_barrier

    block, turned = call(block_kernel, [full, full], unitaries, name="block")
    turned_other = permute(turned, cores)
    chip, plane = call(chip_kernel, [full, full[1:]], turned, turned_other, name="chip")
    near_chip = permute(plane, chips)
    far_chip = permute(near_chip, cores)
    window, own, other = call(window_kernel, [full, strip, strip], chip, near_chip, far_chip, name="window")

    one, one_other = permute(own, twins), permute(other, twins)
    (before,) = call(
        before_kernel, [(2, *full)], unitaries, block, turned_other, near_chip, far_chip, name="before"
    )
    one, before = tie((one, before))
    (both,) = call(extend_kernel, [strip], one, window, name="extend")
    two = permute(both, one_two)
    (both_other,) = call(extend_kernel, [strip], one_other, window, name="extend_other")
    three_other = permute(both_other, one_three)
    three = permute(two, twins)
    two_other = permute(both_other, one_two)

    (across,) = call(merge_kernel, [strip], one_other, two_other, three_other, name="merge_across")
    far_across = permute(across, cores)
    three, across = tie((three, across))
    (near,) = call(merge_kernel, [strip], one, two, three, name="merge_near")
    far = permute(near, cores)
    one, one_other, _ = tie((one, one_other, both_other))
    (left,) = call(
        left_kernel, [(2, *full)], before, one, one_other, permute(one, cores), permute(one_other, cores), name="left"
    )
    scratch = pltpu.VMEM((2, 2, width, width // 2), F32), pltpu.SemaphoreType.DMA((2,))
    shape = [unitaries.shape]
    (out,) = call(near_kernel, shape, left, near, across, name="near", scratch=scratch, hbm_out=True)
    (out,) = call(far_kernel, shape, out, left, far, far_across, name="far", scratch=scratch, hbm_out=True, alias=0)
    return out


def multiply(left, right):
    def body(a, b, out):
        put(out, product(pair(a), pair(b)))

    return call(body, [right.shape], left, right, name="multiply")[0]


def scan(value, axis):
    count, mine = lax.axis_size(axis), lax.axis_index(axis)
    width = value.shape[-1]
    one = jnp.stack([jnp.eye(width, dtype=F32), jnp.zeros((width, width), F32)])
    shifted = lax.ppermute(value, axis, [(i, i + 1) for i in range(count - 1)])
    running = jnp.where(mine >= 1, shifted, one)
    step = 1
    while step < count - 1:
        arrived = lax.ppermute(running, axis, [(i, i + step) for i in range(count - step)])
        running = multiply(running, jnp.where(mine >= step, arrived, one))
        step *= 2
    return running


def general(unitaries):
    own = unitaries[0, 0]
    count = lax.axis_size("tm")
    block = multiply(own[1], own[0])
    before = scan(block, "tm")
    through = multiply(block, before)
    step, mine = 1, lax.axis_index("tm")
    total = through
    while step < count:
        pairs = [(count - 1 - i, count - 1 - i - step) for i in range(min(step, count - step))]
        arrived = lax.ppermute(total, "tm", pairs)
        behind = count - 1 - mine
        total = jnp.where((behind >= step) & (behind < 2 * step), arrived, total)
        step *= 2
    offset = multiply(before, scan(total, "win"))
    first = multiply(own[0], offset)
    return jnp.stack([first, multiply(own[1], first)])[None, None]


def solution(mesh):
    spec = P(("groups", "win"), "tm", None, None, None, None)
    plain = mesh.shape["tm"] == 4 and mesh.shape["win"] == 4
    return jax.shard_map(
        small if plain else general,
        mesh=mesh,
        in_specs=(spec,),
        out_specs=spec,
        check_vma=False,
    )
```

```python
import functools

import jax
import jax.numpy as jnp
from jax import lax
from jax.experimental import pallas as pl
from jax.experimental.pallas import tpu as pltpu
from jax.sharding import PartitionSpec as P

F32 = jnp.float32
AXES = ("tm", "win")
NN = (((1,), (0,)), ((), ()))
NT = (((1,), (1,)), ((), ()))


def halves(x):
    high = x.astype(jnp.bfloat16)
    return high, (x - high.astype(F32)).astype(jnp.bfloat16)


def product(left, right, dims=NN):
    (lr, lrl), (li, lil) = halves(left[0]), halves(left[1])
    (rr, rrl), (ri, ril) = halves(right[0]), halves(right[1])
    dot = functools.partial(
        lax.dot_general, dimension_numbers=dims, preferred_element_type=F32
    )

    def real(a, al, b, bl):
        return dot(a, b) + (dot(a, bl) + dot(al, b))

    return (
        real(lr, lrl, rr, rrl) - real(li, lil, ri, ril),
        real(lr, lrl, ri, ril) + real(li, lil, rr, rrl),
    )


def pick(condition, yes, no):
    return tuple(jnp.where(condition, a, b) for a, b in zip(yes, no, strict=True))


def pair(ref):
    return ref[0], ref[1]


def put(ref, value):
    ref[0] = value[0]
    ref[1] = value[1]


def identity(width):
    rows = lax.broadcasted_iota(jnp.int32, (width, width), 0)
    columns = lax.broadcasted_iota(jnp.int32, (width, width), 1)
    one = (rows == columns).astype(F32)
    return one, jnp.zeros_like(one)


def call(body, outs, *operands, name, scratch=(), hbm_out=False, alias=None):
    whole, far = pl.BlockSpec(memory_space=pltpu.VMEM), pl.BlockSpec(memory_space=pl.ANY)
    shapes = [out if isinstance(out, jax.ShapeDtypeStruct) else jax.ShapeDtypeStruct(out, F32) for out in outs]
    return pl.pallas_call(
        body,
        out_shape=shapes,
        in_specs=[far if i == alias else whole for i in range(len(operands))],
        out_specs=[far if hbm_out and i == 0 else whole for i in range(len(outs))],
        input_output_aliases={} if alias is None else {alias: 0},
        scratch_shapes=list(scratch),
        compiler_params=pltpu.CompilerParams(vmem_limit_bytes=32 << 20),
        name=name,
    )(*operands)


def place():
    t, w = lax.axis_index("tm"), lax.axis_index("win")
    return t // 2, t % 2, w


def block_kernel(u, block, turned):
    b = product(pair(u[0, 0, 1]), pair(u[0, 0, 0]))
    put(block, b)
    put(turned, (b[0].T, b[1].T))


def chip_kernel(mine, theirs, chip, plane):
    _, k, _ = place()
    first = pick(k == 0, pair(mine), pair(theirs))
    second = pick(k == 0, pair(theirs), pair(mine))
    value = product(first, second)
    put(chip, value)
    plane[...] = jnp.where(k == 0, value[0], value[1])


def ordered(x, k, chip, near, far):
    mine = pair(chip)
    other = pick(k == 0, (near[...], far[...]), (far[...], near[...]))
    return pick(x == 0, mine, other), pick(x == 0, other, mine)


def strips_kernel(chip, near, far, own, other, scratch):
    x, k, w = place()

    @pl.when(w % 2 == 0)
    def _():
        one, two = ordered(x, k, chip, near, far)
        put(scratch, one)
        rows = own.shape[1]
        half = scratch[:, pl.ds(pl.multiple_of(2 * k * rows, 2 * rows), 2 * rows), :]
        value = product((half[0], half[1]), two)
        top, low = tuple(v[:rows] for v in value), tuple(v[rows:] for v in value)
        put(own, pick(x == 0, top, low))
        put(other, pick(x == 0, low, top))


def window_kernel(chip, near, far, window):
    x, k, w = place()

    @pl.when(w == 1)
    def _():
        put(window, product(*ordered(x, k, chip, near, far)))


def extend_kernel(piece, window, out):
    _, _, w = place()

    @pl.when(w == 1)
    def _():
        put(out, product(pair(piece), pair(window)))


def stack(upper, lower):
    return tuple(jnp.concatenate([a, b], axis=0) for a, b in zip(upper, lower, strict=True))


def half(x, near, across):
    near, across = pair(near), pair(across)
    return stack(pick(x == 0, near, across), pick(x == 0, across, near))


def whole(near, across, far, far_across):
    x, k, _ = place()
    mine, theirs = half(x, near, across), half(x, far, far_across)
    return stack(pick(k == 0, mine, theirs), pick(k == 0, theirs, mine))


def before_kernel(u, block, turned, near, far, out):
    x, k, _ = place()
    one = identity(block.shape[-1])
    other = pick(k == 0, (near[...], far[...]), (far[...], near[...]))
    before = product(pick(x == 1, other, one), pick(k == 1, pair(turned), one))
    put(out.at[0], product(pair(u[0, 0, 0]), before, NT))
    put(out.at[1], product(pair(block), before, NT))


def left_kernel(before, near, across, far, far_across, high, low):
    _, _, w = place()

    def store(slot, value):
        for plane in range(2):
            high[slot, plane], low[slot, plane] = halves(value[plane])

    @pl.when(w == 3)
    def _():
        window = whole(near, across, far, far_across)
        for slot in range(2):
            store(slot, product(pair(before[slot]), window, NT))

    @pl.when((w == 1) | (w == 2))
    def _():
        for slot in range(2):
            store(slot, pair(before[slot]))


def merge_kernel(one, two, three, out):
    _, _, w = place()
    out[...] = jnp.where(w == 1, one[...], jnp.where(w == 2, two[...], three[...]))


def columns_of(high, low, slot, offset):
    width = offset[0].shape[0] // 2
    dot = functools.partial(lax.dot_general, dimension_numbers=NT, preferred_element_type=F32)
    parts = []
    for plane in range(2):
        a, al = high[slot, plane], low[slot, plane]
        parts.append(dot(a, offset[0]) + (dot(a, offset[1]) + dot(al, offset[0])))
    real, imag = parts
    return real[:, :width] - imag[:, width:], real[:, width:] + imag[:, :width]


def near_kernel(high, low, early, late, out):
    x, _, w = place()

    @pl.when(w != 0)
    def _():
        offset = halves(jnp.concatenate(half(jnp.where(w == 3, 1 - x, x), early, late), axis=0))
        for slot in range(2):
            put(out.at[slot], columns_of(high, low, slot, offset))


def far_kernel(before, near, high, low, early, late, out, far, sems):
    x, k, w = place()
    width = near.shape[-1]

    @pl.when(w == 0)
    def _():
        copies = [pltpu.make_async_copy(before.at[s], out.at[0, 0, s], sems.at[s, 0]) for s in range(2)]
        for copy in copies:
            copy.start()
        for copy in copies:
            copy.wait()

    @pl.when(w != 0)
    def _():
        def start(columns, slot, core, which):
            at = pl.ds(pl.multiple_of(core * width, width), width)
            copy = pltpu.make_async_copy(columns.at[slot], out.at[0, 0, slot, :, :, at], sems.at[slot, which])
            copy.start()
            return copy

        copies = [start(near, slot, k, 0) for slot in range(2)]
        offset = halves(jnp.concatenate(half(jnp.where(w == 3, 1 - x, x), early, late), axis=0))
        for slot in range(2):
            put(far.at[slot], columns_of(high, low, slot, offset))
            copies.append(start(far, slot, 1 - k, 1))
        for copy in copies:
            copy.wait()


def permute(value, pairs):
    windows = lax.axis_size("win")
    flat = [(a * windows + b, c * windows + d) for (a, b), (c, d) in pairs]
    return lax.ppermute(value, AXES, flat)


def small(unitaries):
    width = unitaries.shape[-1]
    full, strip = (2, width, width), (2, width // 4, width)
    spots = [(t, v) for t in range(4) for v in range(4)]
    cores = [((t, v), (t ^ 1, v)) for t, v in spots]
    chips = [((t, v), (t ^ 2, v)) for t, v in spots]
    twins = [((t, v), (t, v ^ 1)) for t, v in spots]
    one_two = [((t, 1), (t, 2)) for t in range(4)]
    two_three = [((t, 2), (t, 3)) for t in range(4)]
    one_three = [((t, 1), (t, 3)) for t in range(4)]
    tie = lax.optimization_barrier

    block, turned = call(block_kernel, [full, full], unitaries, name="block")
    turned_other = permute(turned, cores)
    chip, plane = call(chip_kernel, [full, full[1:]], turned, turned_other, name="chip")
    near_chip = permute(plane, chips)
    far_chip = permute(near_chip, cores)
    own, other = call(
        strips_kernel, [strip, strip], chip, near_chip, far_chip, name="strips", scratch=[pltpu.VMEM(full, F32)]
    )
    one = permute(own, twins)
    (before,) = call(
        before_kernel, [(2, *full)], unitaries, block, turned_other, near_chip, far_chip, name="before"
    )
    (window,) = call(window_kernel, [full], chip, near_chip, far_chip, name="window")
    other, before, window = tie((other, before, window))
    one_other = permute(other, twins)
    one, before = tie((one, before))
    (both,) = call(extend_kernel, [strip], one, window, name="extend")
    two = permute(both, one_two)
    (both_other,) = call(extend_kernel, [strip], one_other, window, name="extend_other")
    three_other = permute(both_other, one_three)
    three = permute(two, two_three)
    two_other = permute(both_other, one_two)

    (early,) = call(merge_kernel, [strip], one, two, three_other, name="merge_early")
    far_early = permute(early, cores)
    one, one_other, _ = tie((one, one_other, both_other))
    parts = [jax.ShapeDtypeStruct((2, *full), jnp.bfloat16)] * 2
    high, low = call(
        left_kernel, parts, before, one, one_other, permute(one, cores), permute(one_other, cores), name="left"
    )
    two_other, three, high, early = tie((two_other, three, high, early))
    (late,) = call(merge_kernel, [strip], one_other, two_other, three, name="merge_late")
    far_late = permute(late, cores)
    half_width = (2, 2, width, width // 2)
    (near,) = call(near_kernel, [half_width], high, low, early, late, name="near")
    scratch = pltpu.VMEM(half_width, F32), pltpu.SemaphoreType.DMA((2, 2))
    operands = before, near, high, low, far_early, far_late
    (out,) = call(far_kernel, [unitaries.shape], *operands, name="far", scratch=scratch, hbm_out=True)
    return out


def multiply(left, right):
    def body(a, b, out):
        put(out, product(pair(a), pair(b)))

    return call(body, [right.shape], left, right, name="multiply")[0]


def scan(value, axis):
    count, mine = lax.axis_size(axis), lax.axis_index(axis)
    width = value.shape[-1]
    one = jnp.stack([jnp.eye(width, dtype=F32), jnp.zeros((width, width), F32)])
    shifted = lax.ppermute(value, axis, [(i, i + 1) for i in range(count - 1)])
    running = jnp.where(mine >= 1, shifted, one)
    step = 1
    while step < count - 1:
        arrived = lax.ppermute(running, axis, [(i, i + step) for i in range(count - step)])
        running = multiply(running, jnp.where(mine >= step, arrived, one))
        step *= 2
    return running


def general(unitaries):
    own = unitaries[0, 0]
    count = lax.axis_size("tm")
    block = multiply(own[1], own[0])
    before = scan(block, "tm")
    through = multiply(block, before)
    step, mine = 1, lax.axis_index("tm")
    total = through
    while step < count:
        pairs = [(count - 1 - i, count - 1 - i - step) for i in range(min(step, count - step))]
        arrived = lax.ppermute(total, "tm", pairs)
        behind = count - 1 - mine
        total = jnp.where((behind >= step) & (behind < 2 * step), arrived, total)
        step *= 2
    offset = multiply(before, scan(total, "win"))
    first = multiply(own[0], offset)
    return jnp.stack([first, multiply(own[1], first)])[None, None]


def solution(mesh):
    spec = P(("groups", "win"), "tm", None, None, None, None)
    plain = mesh.shape["tm"] == 4 and mesh.shape["win"] == 4
    return jax.shard_map(
        small if plain else general,
        mesh=mesh,
        in_specs=(spec,),
        out_specs=spec,
        check_vma=False,
    )
```

```python
import functools

import jax
import jax.numpy as jnp
from jax import lax
from jax.experimental import pallas as pl
from jax.experimental.pallas import tpu as pltpu
from jax.sharding import PartitionSpec as P

F32 = jnp.float32
AXES = ("tm", "win")
NN = (((1,), (0,)), ((), ()))
NT = (((1,), (1,)), ((), ()))


def halves(x):
    high = x.astype(jnp.bfloat16)
    return high, (x - high.astype(F32)).astype(jnp.bfloat16)


def product(left, right, dims=NN):
    (lr, lrl), (li, lil) = halves(left[0]), halves(left[1])
    (rr, rrl), (ri, ril) = halves(right[0]), halves(right[1])
    dot = functools.partial(
        lax.dot_general, dimension_numbers=dims, preferred_element_type=F32
    )

    def real(a, al, b, bl):
        return dot(a, b) + (dot(a, bl) + dot(al, b))

    return (
        real(lr, lrl, rr, rrl) - real(li, lil, ri, ril),
        real(lr, lrl, ri, ril) + real(li, lil, rr, rrl),
    )


def pick(condition, yes, no):
    return tuple(jnp.where(condition, a, b) for a, b in zip(yes, no, strict=True))


def pair(ref):
    return ref[0], ref[1]


def put(ref, value):
    ref[0] = value[0]
    ref[1] = value[1]


def identity(width):
    rows = lax.broadcasted_iota(jnp.int32, (width, width), 0)
    columns = lax.broadcasted_iota(jnp.int32, (width, width), 1)
    one = (rows == columns).astype(F32)
    return one, jnp.zeros_like(one)


def call(body, outs, *operands, name, scratch=(), hbm_out=False, alias=None):
    whole, far = pl.BlockSpec(memory_space=pltpu.VMEM), pl.BlockSpec(memory_space=pl.ANY)
    shapes = [out if isinstance(out, jax.ShapeDtypeStruct) else jax.ShapeDtypeStruct(out, F32) for out in outs]
    return pl.pallas_call(
        body,
        out_shape=shapes,
        in_specs=[far if i == alias else whole for i in range(len(operands))],
        out_specs=[far if hbm_out and i == 0 else whole for i in range(len(outs))],
        input_output_aliases={} if alias is None else {alias: 0},
        scratch_shapes=list(scratch),
        compiler_params=pltpu.CompilerParams(vmem_limit_bytes=32 << 20),
        name=name,
    )(*operands)


def place():
    t, w = lax.axis_index("tm"), lax.axis_index("win")
    return t // 2, t % 2, w


def block_kernel(u, block, turned):
    b = product(pair(u[0, 0, 1]), pair(u[0, 0, 0]))
    put(block, b)
    put(turned, (b[0].T, b[1].T))


def chip_kernel(mine, theirs, chip, plane):
    _, k, _ = place()
    first = pick(k == 0, pair(mine), pair(theirs))
    second = pick(k == 0, pair(theirs), pair(mine))
    value = product(first, second)
    put(chip, value)
    plane[...] = jnp.where(k == 0, value[0], value[1])


def ordered(x, k, chip, near, far):
    mine = pair(chip)
    other = pick(k == 0, (near[...], far[...]), (far[...], near[...]))
    return pick(x == 0, mine, other), pick(x == 0, other, mine)


def strips_kernel(chip, near, far, own, other, scratch):
    x, k, w = place()

    @pl.when(w % 2 == 0)
    def _():
        one, two = ordered(x, k, chip, near, far)
        put(scratch, one)
        rows = own.shape[1]
        half = scratch[:, pl.ds(pl.multiple_of(2 * k * rows, 2 * rows), 2 * rows), :]
        value = product((half[0], half[1]), two)
        top, low = tuple(v[:rows] for v in value), tuple(v[rows:] for v in value)
        put(own, pick(x == 0, top, low))
        put(other, pick(x == 0, low, top))


def window_kernel(chip, near, far, window):
    x, k, w = place()

    @pl.when(w == 1)
    def _():
        put(window, product(*ordered(x, k, chip, near, far)))


def extend_kernel(piece, window, own, out):
    _, _, w = place()

    @pl.when(w == 2)
    def _():
        out[...] = own[...]

    @pl.when(w == 1)
    def _():
        put(out, product(pair(piece), pair(window)))


def stack(upper, lower):
    return tuple(jnp.concatenate([a, b], axis=0) for a, b in zip(upper, lower, strict=True))


def half(x, near, across):
    near, across = pair(near), pair(across)
    return stack(pick(x == 0, near, across), pick(x == 0, across, near))


def whole(near, across, far, far_across):
    x, k, _ = place()
    mine, theirs = half(x, near, across), half(x, far, far_across)
    return stack(pick(k == 0, mine, theirs), pick(k == 0, theirs, mine))


def before_kernel(u, block, turned, near, far, out):
    x, k, _ = place()
    one = identity(block.shape[-1])
    other = pick(k == 0, (near[...], far[...]), (far[...], near[...]))
    before = product(pick(x == 1, other, one), pick(k == 1, pair(turned), one))
    put(out.at[0], product(pair(u[0, 0, 0]), before, NT))
    put(out.at[1], product(pair(block), before, NT))


def left_kernel(before, near, across, far, far_across, high, low):
    _, _, w = place()

    def store(slot, value):
        for plane in range(2):
            high[slot, plane], low[slot, plane] = halves(value[plane])

    @pl.when(w == 3)
    def _():
        window = whole(near, across, far, far_across)
        for slot in range(2):
            store(slot, product(pair(before[slot]), window, NT))

    @pl.when((w == 1) | (w == 2))
    def _():
        for slot in range(2):
            store(slot, pair(before[slot]))


def merge_kernel(one, two, three, out):
    _, _, w = place()
    out[...] = jnp.where(w == 1, one[...], jnp.where(w == 2, two[...], three[...]))


def columns_of(high, low, slot, offset):
    width = offset[0].shape[0] // 2
    dot = functools.partial(lax.dot_general, dimension_numbers=NT, preferred_element_type=F32)
    parts = []
    for plane in range(2):
        a, al = high[slot, plane], low[slot, plane]
        parts.append(dot(a, offset[0]) + (dot(a, offset[1]) + dot(al, offset[0])))
    real, imag = parts
    return real[:, :width] - imag[:, width:], real[:, width:] + imag[:, :width]


def near_kernel(high, low, early, late, out):
    x, _, w = place()

    @pl.when(w != 0)
    def _():
        offset = halves(jnp.concatenate(half(jnp.where(w == 3, 1 - x, x), early, late), axis=0))
        for slot in range(2):
            put(out.at[slot], columns_of(high, low, slot, offset))


def far_kernel(before, near, high, low, early, late, out, far, sems):
    x, k, w = place()
    width = near.shape[-1]

    @pl.when(w == 0)
    def _():
        copies = [pltpu.make_async_copy(before.at[s], out.at[0, 0, s], sems.at[s, 0]) for s in range(2)]
        for copy in copies:
            copy.start()
        for copy in copies:
            copy.wait()

    @pl.when(w != 0)
    def _():
        def start(columns, slot, core, which):
            at = pl.ds(pl.multiple_of(core * width, width), width)
            copy = pltpu.make_async_copy(columns.at[slot], out.at[0, 0, slot, :, :, at], sems.at[slot, which])
            copy.start()
            return copy

        copies = [start(near, slot, k, 0) for slot in range(2)]
        offset = halves(jnp.concatenate(half(jnp.where(w == 3, 1 - x, x), early, late), axis=0))
        for slot in range(2):
            put(far.at[slot], columns_of(high, low, slot, offset))
            copies.append(start(far, slot, 1 - k, 1))
        for copy in copies:
            copy.wait()


def permute(value, pairs):
    windows = lax.axis_size("win")
    flat = [(a * windows + b, c * windows + d) for (a, b), (c, d) in pairs]
    return lax.ppermute(value, AXES, flat)


def small(unitaries):
    width = unitaries.shape[-1]
    full, strip = (2, width, width), (2, width // 4, width)
    spots = [(t, v) for t in range(4) for v in range(4)]
    cores = [((t, v), (t ^ 1, v)) for t, v in spots]
    chips = [((t, v), (t ^ 2, v)) for t, v in spots]
    twins = [((t, v), (t, v ^ 1)) for t, v in spots]
    one_two = [((t, 1), (t, 2)) for t in range(4)]
    zero_one = [((t, 0), (t, 1)) for t in range(4)]
    two_three = [((t, 2), (t, 3)) for t in range(4)]
    onward = [((t, v), (t, (v + 1) % 4)) for t, v in spots]
    one_three = [((t, 1), (t, 3)) for t in range(4)]
    tie = lax.optimization_barrier

    block, turned = call(block_kernel, [full, full], unitaries, name="block")
    turned_other = permute(turned, cores)
    chip, plane = call(chip_kernel, [full, full[1:]], turned, turned_other, name="chip")
    near_chip = permute(plane, chips)
    far_chip = permute(near_chip, cores)
    own, other = call(
        strips_kernel, [strip, strip], chip, near_chip, far_chip, name="strips", scratch=[pltpu.VMEM(full, F32)]
    )
    one = permute(own, twins)
    (window,) = call(window_kernel, [full], chip, near_chip, far_chip, name="window")
    other, window = tie((other, window))
    one_other = permute(other, zero_one)
    (both,) = call(extend_kernel, [strip], one, window, other, name="extend")
    two = permute(both, onward)
    (both_other,) = call(extend_kernel, [strip], one_other, window, other, name="extend_other")
    three_other = permute(both_other, one_three)
    three = permute(two, two_three)
    two_other = permute(both_other, one_two)
    own, _ = tie((one, two))
    strips = own, two, permute(own, cores), permute(two, cores)
    far_chip, _ = tie((far_chip, two))
    (before,) = call(
        before_kernel, [(2, *full)], unitaries, block, turned_other, near_chip, far_chip, name="before"
    )
    three_other, before = tie((three_other, before))
    (early,) = call(merge_kernel, [strip], one, two, three_other, name="merge_early")
    far_early = permute(early, cores)
    parts = [jax.ShapeDtypeStruct((2, *full), jnp.bfloat16)] * 2
    high, low = call(left_kernel, parts, before, *strips, name="left")
    two_other, early = tie((two_other, early))
    (other,) = call(merge_kernel, [strip], one_other, two_other, two_other, name="merge_other")
    three, other, high = tie((three, other, high))
    (late,) = call(merge_kernel, [strip], other, other, three, name="merge_late")
    far_late = permute(late, cores)
    half_width = (2, 2, width, width // 2)
    (near,) = call(near_kernel, [half_width], high, low, early, late, name="near")
    scratch = pltpu.VMEM(half_width, F32), pltpu.SemaphoreType.DMA((2, 2))
    operands = before, near, high, low, far_early, far_late
    (out,) = call(far_kernel, [unitaries.shape], *operands, name="far", scratch=scratch, hbm_out=True)
    return out


def multiply(left, right):
    def body(a, b, out):
        put(out, product(pair(a), pair(b)))

    return call(body, [right.shape], left, right, name="multiply")[0]


def scan(value, axis):
    count, mine = lax.axis_size(axis), lax.axis_index(axis)
    width = value.shape[-1]
    one = jnp.stack([jnp.eye(width, dtype=F32), jnp.zeros((width, width), F32)])
    shifted = lax.ppermute(value, axis, [(i, i + 1) for i in range(count - 1)])
    running = jnp.where(mine >= 1, shifted, one)
    step = 1
    while step < count - 1:
        arrived = lax.ppermute(running, axis, [(i, i + step) for i in range(count - step)])
        running = multiply(running, jnp.where(mine >= step, arrived, one))
        step *= 2
    return running


def general(unitaries):
    own = unitaries[0, 0]
    count = lax.axis_size("tm")
    block = multiply(own[1], own[0])
    before = scan(block, "tm")
    through = multiply(block, before)
    step, mine = 1, lax.axis_index("tm")
    total = through
    while step < count:
        pairs = [(count - 1 - i, count - 1 - i - step) for i in range(min(step, count - step))]
        arrived = lax.ppermute(total, "tm", pairs)
        behind = count - 1 - mine
        total = jnp.where((behind >= step) & (behind < 2 * step), arrived, total)
        step *= 2
    offset = multiply(before, scan(total, "win"))
    first = multiply(own[0], offset)
    return jnp.stack([first, multiply(own[1], first)])[None, None]


def solution(mesh):
    spec = P(("groups", "win"), "tm", None, None, None, None)
    plain = mesh.shape["tm"] == 4 and mesh.shape["win"] == 4
    return jax.shard_map(
        small if plain else general,
        mesh=mesh,
        in_specs=(spec,),
        out_specs=spec,
        check_vma=False,
    )
```

```python
import functools

import jax
import jax.numpy as jnp
from jax import lax
from jax.experimental import pallas as pl
from jax.experimental.pallas import tpu as pltpu
from jax.sharding import PartitionSpec as P

F32 = jnp.float32
AXES = ("tm", "win")
NN = (((1,), (0,)), ((), ()))
NT = (((1,), (1,)), ((), ()))


def halves(x):
    high = x.astype(jnp.bfloat16)
    return high, (x - high.astype(F32)).astype(jnp.bfloat16)


def product(left, right, dims=NN):
    (lr, lrl), (li, lil) = halves(left[0]), halves(left[1])
    (rr, rrl), (ri, ril) = halves(right[0]), halves(right[1])
    dot = functools.partial(
        lax.dot_general, dimension_numbers=dims, preferred_element_type=F32
    )

    def real(a, al, b, bl):
        return dot(a, b) + (dot(a, bl) + dot(al, b))

    return (
        real(lr, lrl, rr, rrl) - real(li, lil, ri, ril),
        real(lr, lrl, ri, ril) + real(li, lil, rr, rrl),
    )


def pick(condition, yes, no):
    return tuple(jnp.where(condition, a, b) for a, b in zip(yes, no, strict=True))


def pair(ref):
    return ref[0], ref[1]


def put(ref, value):
    ref[0] = value[0]
    ref[1] = value[1]


def identity(width):
    rows = lax.broadcasted_iota(jnp.int32, (width, width), 0)
    columns = lax.broadcasted_iota(jnp.int32, (width, width), 1)
    one = (rows == columns).astype(F32)
    return one, jnp.zeros_like(one)


def call(body, outs, *operands, name, scratch=(), hbm_out=False, alias=None):
    whole, far = pl.BlockSpec(memory_space=pltpu.VMEM), pl.BlockSpec(memory_space=pl.ANY)
    shapes = [out if isinstance(out, jax.ShapeDtypeStruct) else jax.ShapeDtypeStruct(out, F32) for out in outs]
    return pl.pallas_call(
        body,
        out_shape=shapes,
        in_specs=[far if i == alias else whole for i in range(len(operands))],
        out_specs=[far if hbm_out and i == 0 else whole for i in range(len(outs))],
        input_output_aliases={} if alias is None else {alias: 0},
        scratch_shapes=list(scratch),
        compiler_params=pltpu.CompilerParams(vmem_limit_bytes=32 << 20),
        name=name,
    )(*operands)


def place():
    t, w = lax.axis_index("tm"), lax.axis_index("win")
    return t // 2, t % 2, w


def block_kernel(u, block, turned):
    b = product(pair(u[0, 0, 1]), pair(u[0, 0, 0]))
    put(block, b)
    put(turned, (b[0].T, b[1].T))


def chip_kernel(mine, theirs, chip, plane):
    _, k, _ = place()
    first = pick(k == 0, pair(mine), pair(theirs))
    second = pick(k == 0, pair(theirs), pair(mine))
    value = product(first, second)
    put(chip, value)
    plane[...] = jnp.where(k == 0, value[0], value[1])


def ordered(x, k, chip, near, far):
    mine = pair(chip)
    other = pick(k == 0, (near[...], far[...]), (far[...], near[...]))
    return pick(x == 0, mine, other), pick(x == 0, other, mine)


def strips_kernel(chip, near, far, own, other, scratch):
    x, k, w = place()

    @pl.when(w % 2 == 0)
    def _():
        one, two = ordered(x, k, chip, near, far)
        put(scratch, one)
        rows = own.shape[1]
        half = scratch[:, pl.ds(pl.multiple_of(2 * k * rows, 2 * rows), 2 * rows), :]
        value = product((half[0], half[1]), two)
        top, low = tuple(v[:rows] for v in value), tuple(v[rows:] for v in value)
        put(own, pick(x == 0, top, low))
        put(other, pick(x == 0, low, top))


def window_kernel(chip, near, far, window):
    x, k, w = place()

    @pl.when(w == 1)
    def _():
        put(window, product(*ordered(x, k, chip, near, far)))


def extend_kernel(piece, window, own, out):
    _, _, w = place()

    @pl.when(w == 2)
    def _():
        out[...] = own[...]

    @pl.when(w == 1)
    def _():
        put(out, product(pair(piece), pair(window)))


def stack(upper, lower):
    return tuple(jnp.concatenate([a, b], axis=0) for a, b in zip(upper, lower, strict=True))


def half(x, near, across):
    near, across = pair(near), pair(across)
    return stack(pick(x == 0, near, across), pick(x == 0, across, near))


def whole(near, across, far, far_across):
    x, k, _ = place()
    mine, theirs = half(x, near, across), half(x, far, far_across)
    return stack(pick(k == 0, mine, theirs), pick(k == 0, theirs, mine))


def before_kernel(u, block, turned, near, far, out):
    x, k, _ = place()
    one = identity(block.shape[-1])
    other = pick(k == 0, (near[...], far[...]), (far[...], near[...]))
    before = product(pick(x == 1, other, one), pick(k == 1, pair(turned), one))
    put(out.at[0], product(pair(u[0, 0, 0]), before, NT))
    put(out.at[1], product(pair(block), before, NT))


def left_kernel(before, near, across, high, low, *, mine):
    x, k, w = place()
    width = high.shape[-1]

    @pl.when(w == 3)
    def _():
        strips = half(x, near, across)
        for slot in range(2):
            value = columns_of(*parts_of(before, slot), 0, halves(jnp.concatenate(strips, axis=0)))
            for plane in range(2):
                high[slot, plane], low[slot, plane] = halves(value[plane])

    @pl.when((w == 1) | (w == 2))
    def _():
        core = k if mine else 1 - k
        for slot in range(2):
            for plane in range(2):
                value = before[slot, plane, :, pl.ds(pl.multiple_of(core * width, width), width)]
                high[slot, plane], low[slot, plane] = halves(value)


def parts_of(ref, slot):
    planes = [halves(ref[slot, plane]) for plane in range(2)]
    return tuple({(0, plane): planes[plane][part] for plane in range(2)} for part in range(2))


def merge_kernel(one, two, three, out):
    _, _, w = place()
    out[...] = jnp.where(w == 1, one[...], jnp.where(w == 2, two[...], three[...]))


def columns_of(high, low, slot, offset):
    width = offset[0].shape[0] // 2
    dot = functools.partial(lax.dot_general, dimension_numbers=NT, preferred_element_type=F32)
    parts = []
    for plane in range(2):
        a, al = high[slot, plane], low[slot, plane]
        parts.append(dot(a, offset[0]) + (dot(a, offset[1]) + dot(al, offset[0])))
    real, imag = parts
    return real[:, :width] - imag[:, width:], real[:, width:] + imag[:, :width]


def joined(k, mine, theirs):
    def plane(slot, index):
        a, b = mine[slot, index], theirs[slot, index]
        return jnp.concatenate([jnp.where(k == 0, a, b), jnp.where(k == 0, b, a)], axis=1)

    return {(slot, index): plane(slot, index) for slot in range(2) for index in range(2)}


def near_kernel(high, low, far_high, far_low, early, late, out, whole_high, whole_low):
    x, k, w = place()

    @pl.when(w != 0)
    def _():
        both_high, both_low = joined(k, high, far_high), joined(k, low, far_low)
        for slot in range(2):
            for plane in range(2):
                whole_high[slot, plane], whole_low[slot, plane] = both_high[slot, plane], both_low[slot, plane]
        offset = halves(jnp.concatenate(half(jnp.where(w == 3, 1 - x, x), early, late), axis=0))
        for slot in range(2):
            put(out.at[slot], columns_of(both_high, both_low, slot, offset))


def far_kernel(before, near, high, low, early, late, out, far, sems):
    x, k, w = place()
    width = near.shape[-1]

    @pl.when(w == 0)
    def _():
        copies = [pltpu.make_async_copy(before.at[s], out.at[0, 0, s], sems.at[s, 0]) for s in range(2)]
        for copy in copies:
            copy.start()
        for copy in copies:
            copy.wait()

    @pl.when(w != 0)
    def _():
        def start(columns, slot, core, which):
            at = pl.ds(pl.multiple_of(core * width, width), width)
            copy = pltpu.make_async_copy(columns.at[slot], out.at[0, 0, slot, :, :, at], sems.at[slot, which])
            copy.start()
            return copy

        copies = [start(near, slot, k, 0) for slot in range(2)]
        offset = halves(jnp.concatenate(half(jnp.where(w == 3, 1 - x, x), early, late), axis=0))
        for slot in range(2):
            put(far.at[slot], columns_of(high, low, slot, offset))
            copies.append(start(far, slot, 1 - k, 1))
        for copy in copies:
            copy.wait()


def permute(value, pairs):
    windows = lax.axis_size("win")
    flat = [(a * windows + b, c * windows + d) for (a, b), (c, d) in pairs]
    return lax.ppermute(value, AXES, flat)


def small(unitaries):
    width = unitaries.shape[-1]
    full, strip = (2, width, width), (2, width // 4, width)
    spots = [(t, v) for t in range(4) for v in range(4)]
    cores = [((t, v), (t ^ 1, v)) for t, v in spots]
    chips = [((t, v), (t ^ 2, v)) for t, v in spots]
    twins = [((t, v), (t, v ^ 1)) for t, v in spots]
    one_two = [((t, 1), (t, 2)) for t in range(4)]
    zero_one = [((t, 0), (t, 1)) for t in range(4)]
    two_three = [((t, 2), (t, 3)) for t in range(4)]
    onward = [((t, v), (t, (v + 1) % 4)) for t, v in spots]
    one_three = [((t, 1), (t, 3)) for t in range(4)]
    tie = lax.optimization_barrier

    block, turned = call(block_kernel, [full, full], unitaries, name="block")
    turned_other = permute(turned, cores)
    chip, plane = call(chip_kernel, [full, full[1:]], turned, turned_other, name="chip")
    near_chip = permute(plane, chips)
    far_chip = permute(near_chip, cores)
    own, other = call(
        strips_kernel, [strip, strip], chip, near_chip, far_chip, name="strips", scratch=[pltpu.VMEM(full, F32)]
    )
    one = permute(own, twins)
    (window,) = call(window_kernel, [full], chip, near_chip, far_chip, name="window")
    other, window = tie((other, window))
    one_other = permute(other, zero_one)
    (both,) = call(extend_kernel, [strip], one, window, other, name="extend")
    two = permute(both, onward)
    (both_other,) = call(extend_kernel, [strip], one_other, window, other, name="extend_other")
    three_other = permute(both_other, one_three)
    three = permute(two, two_three)
    two_other = permute(both_other, one_two)
    own, past = tie((one, two))
    far_own, far_past = permute(own, cores), permute(past, cores)
    far_chip, _ = tie((far_chip, two))
    (before,) = call(
        before_kernel, [(2, *full)], unitaries, block, turned_other, near_chip, far_chip, name="before"
    )
    three_other, before = tie((three_other, before))
    parts = [jax.ShapeDtypeStruct((2, 2, width, width // 2), jnp.bfloat16)] * 2
    high, low = call(functools.partial(left_kernel, mine=True), parts, before, own, past, name="left_near")
    three_other, high = tie((three_other, high))
    (early,) = call(merge_kernel, [strip], one, two, three_other, name="merge_early")
    far_early = permute(early, cores)
    two_other, early = tie((two_other, early))
    (other,) = call(merge_kernel, [strip], one_other, two_other, two_other, name="merge_other")
    three, other = tie((three, other))
    (late,) = call(merge_kernel, [strip], other, other, three, name="merge_late")
    far_late = permute(late, cores)
    theirs = call(functools.partial(left_kernel, mine=False), parts, before, far_own, far_past, name="left_far")
    half_width, both = (2, 2, width, width // 2), jax.ShapeDtypeStruct((2, *full), jnp.bfloat16)
    near, high, low = call(near_kernel, [half_width, both, both], high, low, *theirs, early, late, name="near")
    scratch = pltpu.VMEM(half_width, F32), pltpu.SemaphoreType.DMA((2, 2))
    operands = before, near, high, low, far_early, far_late
    (out,) = call(far_kernel, [unitaries.shape], *operands, name="far", scratch=scratch, hbm_out=True)
    return out


def multiply(left, right):
    def body(a, b, out):
        put(out, product(pair(a), pair(b)))

    return call(body, [right.shape], left, right, name="multiply")[0]


def scan(value, axis):
    count, mine = lax.axis_size(axis), lax.axis_index(axis)
    width = value.shape[-1]
    one = jnp.stack([jnp.eye(width, dtype=F32), jnp.zeros((width, width), F32)])
    shifted = lax.ppermute(value, axis, [(i, i + 1) for i in range(count - 1)])
    running = jnp.where(mine >= 1, shifted, one)
    step = 1
    while step < count - 1:
        arrived = lax.ppermute(running, axis, [(i, i + step) for i in range(count - step)])
        running = multiply(running, jnp.where(mine >= step, arrived, one))
        step *= 2
    return running


def general(unitaries):
    own = unitaries[0, 0]
    count = lax.axis_size("tm")
    block = multiply(own[1], own[0])
    before = scan(block, "tm")
    through = multiply(block, before)
    step, mine = 1, lax.axis_index("tm")
    total = through
    while step < count:
        pairs = [(count - 1 - i, count - 1 - i - step) for i in range(min(step, count - step))]
        arrived = lax.ppermute(total, "tm", pairs)
        behind = count - 1 - mine
        total = jnp.where((behind >= step) & (behind < 2 * step), arrived, total)
        step *= 2
    offset = multiply(before, scan(total, "win"))
    first = multiply(own[0], offset)
    return jnp.stack([first, multiply(own[1], first)])[None, None]


def solution(mesh):
    spec = P(("groups", "win"), "tm", None, None, None, None)
    plain = mesh.shape["tm"] == 4 and mesh.shape["win"] == 4
    return jax.shard_map(
        small if plain else general,
        mesh=mesh,
        in_specs=(spec,),
        out_specs=spec,
        check_vma=False,
    )
```

```python
import functools

import jax
import jax.numpy as jnp
from jax import lax
from jax.experimental import pallas as pl
from jax.experimental.pallas import tpu as pltpu
from jax.sharding import PartitionSpec as P

F32 = jnp.float32
AXES = ("tm", "win")
NN = (((1,), (0,)), ((), ()))
NT = (((1,), (1,)), ((), ()))


def halves(x):
    high = x.astype(jnp.bfloat16)
    return high, (x - high.astype(F32)).astype(jnp.bfloat16)


def product(left, right, dims=NN):
    (lr, lrl), (li, lil) = halves(left[0]), halves(left[1])
    (rr, rrl), (ri, ril) = halves(right[0]), halves(right[1])
    dot = functools.partial(
        lax.dot_general, dimension_numbers=dims, preferred_element_type=F32
    )

    def real(a, al, b, bl):
        return dot(a, b) + (dot(a, bl) + dot(al, b))

    return (
        real(lr, lrl, rr, rrl) - real(li, lil, ri, ril),
        real(lr, lrl, ri, ril) + real(li, lil, rr, rrl),
    )


def pick(condition, yes, no):
    return tuple(jnp.where(condition, a, b) for a, b in zip(yes, no, strict=True))


def pair(ref):
    return ref[0], ref[1]


def put(ref, value):
    ref[0] = value[0]
    ref[1] = value[1]


def identity(width):
    rows = lax.broadcasted_iota(jnp.int32, (width, width), 0)
    columns = lax.broadcasted_iota(jnp.int32, (width, width), 1)
    one = (rows == columns).astype(F32)
    return one, jnp.zeros_like(one)


def call(body, outs, *operands, name, scratch=(), hbm_out=False, alias=None):
    whole, far = pl.BlockSpec(memory_space=pltpu.VMEM), pl.BlockSpec(memory_space=pl.ANY)
    shapes = [out if isinstance(out, jax.ShapeDtypeStruct) else jax.ShapeDtypeStruct(out, F32) for out in outs]
    return pl.pallas_call(
        body,
        out_shape=shapes,
        in_specs=[far if i == alias else whole for i in range(len(operands))],
        out_specs=[far if hbm_out and i == 0 else whole for i in range(len(outs))],
        input_output_aliases={} if alias is None else {alias: 0},
        scratch_shapes=list(scratch),
        compiler_params=pltpu.CompilerParams(vmem_limit_bytes=32 << 20),
        name=name,
    )(*operands)


def place():
    t, w = lax.axis_index("tm"), lax.axis_index("win")
    return t // 2, t % 2, w


def block_kernel(u, block, turned):
    b = product(pair(u[0, 0, 1]), pair(u[0, 0, 0]))
    put(block, b)
    put(turned, (b[0].T, b[1].T))


def chip_kernel(mine, theirs, chip, plane):
    _, k, _ = place()
    first = pick(k == 0, pair(mine), pair(theirs))
    second = pick(k == 0, pair(theirs), pair(mine))
    value = product(first, second)
    put(chip, value)
    plane[...] = jnp.where(k == 0, value[0], value[1])


def ordered(x, k, chip, near, far):
    mine = pair(chip)
    other = pick(k == 0, (near[...], far[...]), (far[...], near[...]))
    return pick(x == 0, mine, other), pick(x == 0, other, mine)


def strips_kernel(chip, near, far, own, other, scratch):
    x, k, w = place()

    @pl.when(w % 2 == 0)
    def _():
        one, two = ordered(x, k, chip, near, far)
        put(scratch, one)
        rows = own.shape[1]
        half = scratch[:, pl.ds(pl.multiple_of(2 * k * rows, 2 * rows), 2 * rows), :]
        value = product((half[0], half[1]), two)
        top, low = tuple(v[:rows] for v in value), tuple(v[rows:] for v in value)
        put(own, pick(x == 0, top, low))
        put(other, pick(x == 0, low, top))


def window_kernel(chip, near, far, window):
    x, k, w = place()

    @pl.when(w == 1)
    def _():
        put(window, product(*ordered(x, k, chip, near, far)))


def extend_kernel(piece, window, own, out):
    _, _, w = place()

    @pl.when(w == 2)
    def _():
        out[...] = own[...]

    @pl.when(w == 1)
    def _():
        put(out, product(pair(piece), pair(window)))


def stack(upper, lower):
    return tuple(jnp.concatenate([a, b], axis=0) for a, b in zip(upper, lower, strict=True))


def half(x, near, across):
    near, across = pair(near), pair(across)
    return stack(pick(x == 0, near, across), pick(x == 0, across, near))


def whole(near, across, far, far_across):
    x, k, _ = place()
    mine, theirs = half(x, near, across), half(x, far, far_across)
    return stack(pick(k == 0, mine, theirs), pick(k == 0, theirs, mine))


def before_kernel(u, block, turned, near, far, out, high, low):
    x, k, _ = place()
    one = identity(block.shape[-1])
    other = pick(k == 0, (near[...], far[...]), (far[...], near[...]))
    before = product(pick(x == 1, other, one), pick(k == 1, pair(turned), one))
    for slot, left in enumerate((pair(u[0, 0, 0]), pair(block))):
        value = product(left, before, NT)
        put(out.at[slot], value)
        for plane in range(2):
            high[slot, plane], low[slot, plane] = halves(value[plane])


def left_half(before, near, across, core, high, low):
    x, _, w = place()
    width = before[0].shape[-1] // 2

    @pl.when(w == 3)
    def _():
        strips = halves(jnp.concatenate(half(x, near, across), axis=0))
        for slot in range(2):
            value = columns_of(*before, slot, strips)
            for plane in range(2):
                high[slot, plane], low[slot, plane] = halves(value[plane])

    @pl.when((w == 1) | (w == 2))
    def _():
        at = pl.ds(pl.multiple_of(core * width, width), width)
        high[...], low[...] = (part[:, :, :, at] for part in before)


def left_kernel(before_high, before_low, near, across, high, low):
    _, k, _ = place()
    left_half((before_high, before_low), near, across, k, high, low)


def merge_kernel(one, two, three, out):
    _, _, w = place()
    out[...] = jnp.where(w == 1, one[...], jnp.where(w == 2, two[...], three[...]))


def columns_of(high, low, slot, offset):
    width = offset[0].shape[0] // 2
    dot = functools.partial(lax.dot_general, dimension_numbers=NT, preferred_element_type=F32)
    parts = []
    for plane in range(2):
        a, al = high[slot, plane], low[slot, plane]
        parts.append(dot(a, offset[0]) + (dot(a, offset[1]) + dot(al, offset[0])))
    real, imag = parts
    return real[:, :width] - imag[:, width:], real[:, width:] + imag[:, :width]


def joined(k, mine, theirs):
    def plane(slot, index):
        a, b = mine[slot, index], theirs[slot, index]
        return jnp.concatenate([jnp.where(k == 0, a, b), jnp.where(k == 0, b, a)], axis=1)

    return {(slot, index): plane(slot, index) for slot in range(2) for index in range(2)}


def near_kernel(
    before_high, before_low, far_own, far_past, high, low, early, late, out, whole_high, whole_low, far_high, far_low
):
    x, k, w = place()
    left_half((before_high, before_low), far_own, far_past, 1 - k, far_high, far_low)

    @pl.when(w != 0)
    def _():
        both_high, both_low = joined(k, high, far_high), joined(k, low, far_low)
        for slot in range(2):
            for plane in range(2):
                whole_high[slot, plane], whole_low[slot, plane] = both_high[slot, plane], both_low[slot, plane]
        offset = halves(jnp.concatenate(half(jnp.where(w == 3, 1 - x, x), early, late), axis=0))
        for slot in range(2):
            put(out.at[slot], columns_of(both_high, both_low, slot, offset))


def far_kernel(before, near, high, low, early, late, out, far, sems):
    x, k, w = place()
    width = near.shape[-1]

    @pl.when(w == 0)
    def _():
        copies = [pltpu.make_async_copy(before.at[s], out.at[0, 0, s], sems.at[s, 0]) for s in range(2)]
        for copy in copies:
            copy.start()
        for copy in copies:
            copy.wait()

    @pl.when(w != 0)
    def _():
        def start(columns, slot, core, which):
            at = pl.ds(pl.multiple_of(core * width, width), width)
            copy = pltpu.make_async_copy(columns.at[slot], out.at[0, 0, slot, :, :, at], sems.at[slot, which])
            copy.start()
            return copy

        copies = [start(near, slot, k, 0) for slot in range(2)]
        offset = halves(jnp.concatenate(half(jnp.where(w == 3, 1 - x, x), early, late), axis=0))
        for slot in range(2):
            put(far.at[slot], columns_of(high, low, slot, offset))
            copies.append(start(far, slot, 1 - k, 1))
        for copy in copies:
            copy.wait()


def permute(value, pairs):
    windows = lax.axis_size("win")
    flat = [(a * windows + b, c * windows + d) for (a, b), (c, d) in pairs]
    return lax.ppermute(value, AXES, flat)


def small(unitaries):
    width = unitaries.shape[-1]
    full, strip = (2, width, width), (2, width // 4, width)
    spots = [(t, v) for t in range(4) for v in range(4)]
    cores = [((t, v), (t ^ 1, v)) for t, v in spots]
    chips = [((t, v), (t ^ 2, v)) for t, v in spots]
    twins = [((t, v), (t, v ^ 1)) for t, v in spots]
    one_two = [((t, 1), (t, 2)) for t in range(4)]
    zero_one = [((t, 0), (t, 1)) for t in range(4)]
    two_three = [((t, 2), (t, 3)) for t in range(4)]
    onward = [((t, v), (t, (v + 1) % 4)) for t, v in spots]
    one_three = [((t, 1), (t, 3)) for t in range(4)]
    tie = lax.optimization_barrier

    block, turned = call(block_kernel, [full, full], unitaries, name="block")
    turned_other = permute(turned, cores)
    chip, plane = call(chip_kernel, [full, full[1:]], turned, turned_other, name="chip")
    near_chip = permute(plane, chips)
    far_chip = permute(near_chip, cores)
    own, other = call(
        strips_kernel, [strip, strip], chip, near_chip, far_chip, name="strips", scratch=[pltpu.VMEM(full, F32)]
    )
    one = permute(own, twins)
    (window,) = call(window_kernel, [full], chip, near_chip, far_chip, name="window")
    one_other = permute(other, zero_one)
    (both,) = call(extend_kernel, [strip], one, window, other, name="extend")
    two = permute(both, onward)
    (both_other,) = call(extend_kernel, [strip], one_other, window, other, name="extend_other")
    three_other = permute(both_other, one_three)
    three = permute(two, two_three)
    two_other = permute(both_other, one_two)
    own, past = tie((one, two))
    far_own, far_past = permute(own, cores), permute(past, cores)
    far_chip, _ = tie((far_chip, two))
    both = jax.ShapeDtypeStruct((2, *full), jnp.bfloat16)
    operands = unitaries, block, turned_other, near_chip, far_chip
    before, *before_parts = call(before_kernel, [(2, *full), both, both], *operands, name="before")
    three_other, before = tie((three_other, before))
    parts = [jax.ShapeDtypeStruct((2, 2, width, width // 2), jnp.bfloat16)] * 2
    high, low = call(left_kernel, parts, *before_parts, own, past, name="left")
    three_other, high = tie((three_other, high))
    (early,) = call(merge_kernel, [strip], one, two, three_other, name="merge_early")
    far_early = permute(early, cores)
    two_other, early = tie((two_other, early))
    (other,) = call(merge_kernel, [strip], one_other, two_other, two_other, name="merge_other")
    three, other = tie((three, other))
    (late,) = call(merge_kernel, [strip], other, other, three, name="merge_late")
    far_late = permute(late, cores)
    half_width = (2, 2, width, width // 2)
    operands = *before_parts, far_own, far_past, high, low, early, late
    scratch = [pltpu.VMEM(half_width, jnp.bfloat16)] * 2
    near, high, low = call(near_kernel, [half_width, both, both], *operands, name="near", scratch=scratch)
    scratch = pltpu.VMEM(half_width, F32), pltpu.SemaphoreType.DMA((2, 2))
    operands = before, near, high, low, far_early, far_late
    (out,) = call(far_kernel, [unitaries.shape], *operands, name="far", scratch=scratch, hbm_out=True)
    return out


def multiply(left, right):
    def body(a, b, out):
        put(out, product(pair(a), pair(b)))

    return call(body, [right.shape], left, right, name="multiply")[0]


def scan(value, axis):
    count, mine = lax.axis_size(axis), lax.axis_index(axis)
    width = value.shape[-1]
    one = jnp.stack([jnp.eye(width, dtype=F32), jnp.zeros((width, width), F32)])
    shifted = lax.ppermute(value, axis, [(i, i + 1) for i in range(count - 1)])
    running = jnp.where(mine >= 1, shifted, one)
    step = 1
    while step < count - 1:
        arrived = lax.ppermute(running, axis, [(i, i + step) for i in range(count - step)])
        running = multiply(running, jnp.where(mine >= step, arrived, one))
        step *= 2
    return running


def general(unitaries):
    own = unitaries[0, 0]
    count = lax.axis_size("tm")
    block = multiply(own[1], own[0])
    before = scan(block, "tm")
    through = multiply(block, before)
    step, mine = 1, lax.axis_index("tm")
    total = through
    while step < count:
        pairs = [(count - 1 - i, count - 1 - i - step) for i in range(min(step, count - step))]
        arrived = lax.ppermute(total, "tm", pairs)
        behind = count - 1 - mine
        total = jnp.where((behind >= step) & (behind < 2 * step), arrived, total)
        step *= 2
    offset = multiply(before, scan(total, "win"))
    first = multiply(own[0], offset)
    return jnp.stack([first, multiply(own[1], first)])[None, None]


def solution(mesh):
    spec = P(("groups", "win"), "tm", None, None, None, None)
    plain = mesh.shape["tm"] == 4 and mesh.shape["win"] == 4
    return jax.shard_map(
        small if plain else general,
        mesh=mesh,
        in_specs=(spec,),
        out_specs=spec,
        check_vma=False,
    )
```

```python
import functools

import jax
import jax.numpy as jnp
from jax import lax
from jax.experimental import pallas as pl
from jax.experimental.pallas import tpu as pltpu
from jax.sharding import PartitionSpec as P

F32 = jnp.float32
AXES = ("tm", "win")
NN = (((1,), (0,)), ((), ()))
NT = (((1,), (1,)), ((), ()))


def halves(x):
    high = x.astype(jnp.bfloat16)
    return high, (x - high.astype(F32)).astype(jnp.bfloat16)


def product(left, right, dims=NN):
    (lr, lrl), (li, lil) = halves(left[0]), halves(left[1])
    (rr, rrl), (ri, ril) = halves(right[0]), halves(right[1])
    dot = functools.partial(
        lax.dot_general, dimension_numbers=dims, preferred_element_type=F32
    )

    def real(a, al, b, bl):
        return dot(a, b) + (dot(a, bl) + dot(al, b))

    return (
        real(lr, lrl, rr, rrl) - real(li, lil, ri, ril),
        real(lr, lrl, ri, ril) + real(li, lil, rr, rrl),
    )


def real_product(left, right):
    (a, al), (b, bl) = halves(left), halves(right)
    dot = functools.partial(jnp.dot, preferred_element_type=F32)
    return dot(a, b) + (dot(a, bl) + dot(al, b))


def pick(condition, yes, no):
    return tuple(jnp.where(condition, a, b) for a, b in zip(yes, no, strict=True))


def pair(ref):
    return ref[0], ref[1]


def put(ref, value):
    ref[0] = value[0]
    ref[1] = value[1]


def identity(width):
    rows = lax.broadcasted_iota(jnp.int32, (width, width), 0)
    columns = lax.broadcasted_iota(jnp.int32, (width, width), 1)
    one = (rows == columns).astype(F32)
    return one, jnp.zeros_like(one)


def call(body, outs, *operands, name, scratch=(), hbm_out=False, alias=None):
    whole, far = pl.BlockSpec(memory_space=pltpu.VMEM), pl.BlockSpec(memory_space=pl.ANY)
    shapes = [out if isinstance(out, jax.ShapeDtypeStruct) else jax.ShapeDtypeStruct(out, F32) for out in outs]
    return pl.pallas_call(
        body,
        out_shape=shapes,
        in_specs=[far if i == alias else whole for i in range(len(operands))],
        out_specs=[far if hbm_out and i == 0 else whole for i in range(len(outs))],
        input_output_aliases={} if alias is None else {alias: 0},
        scratch_shapes=list(scratch),
        compiler_params=pltpu.CompilerParams(vmem_limit_bytes=32 << 20),
        name=name,
    )(*operands)


def place():
    t, w = lax.axis_index("tm"), lax.axis_index("win")
    return t // 2, t % 2, w


def block_kernel(u, block, turned):
    b = product(pair(u[0, 0, 1]), pair(u[0, 0, 0]))
    put(block, b)
    put(turned, (b[0].T, b[1].T))


def plane_kernel(mine, theirs, plane):
    _, k, _ = place()

    @pl.when(k == 0)
    def _():
        (lr, li), (rr, ri) = pair(mine), pair(theirs)
        plane[...] = real_product(lr, rr) - real_product(li, ri)

    @pl.when(k == 1)
    def _():
        (lr, li), (rr, ri) = pair(theirs), pair(mine)
        plane[...] = real_product(lr, ri) + real_product(li, rr)


def chip_kernel(mine, theirs, plane, chip):
    _, k, _ = place()

    @pl.when(k == 0)
    def _():
        (lr, li), (rr, ri) = pair(mine), pair(theirs)
        put(chip, (plane[...], real_product(lr, ri) + real_product(li, rr)))

    @pl.when(k == 1)
    def _():
        (lr, li), (rr, ri) = pair(theirs), pair(mine)
        put(chip, (real_product(lr, rr) - real_product(li, ri), plane[...]))


def ordered(x, k, chip, near, far):
    mine = pair(chip)
    other = pick(k == 0, (near[...], far[...]), (far[...], near[...]))
    return pick(x == 0, mine, other), pick(x == 0, other, mine)


def strips_kernel(chip, near, far, own, other, scratch):
    x, k, w = place()

    @pl.when(w % 2 == 0)
    def _():
        one, two = ordered(x, k, chip, near, far)
        put(scratch, one)
        rows = own.shape[1]
        half = scratch[:, pl.ds(pl.multiple_of(2 * k * rows, 2 * rows), 2 * rows), :]
        value = product((half[0], half[1]), two)
        top, low = tuple(v[:rows] for v in value), tuple(v[rows:] for v in value)
        put(own, pick(x == 0, top, low))
        put(other, pick(x == 0, low, top))


def window_kernel(chip, near, far, window):
    x, k, w = place()

    @pl.when(w == 1)
    def _():
        put(window, product(*ordered(x, k, chip, near, far)))


def extend_kernel(piece, window, own, out):
    _, _, w = place()

    @pl.when(w == 2)
    def _():
        out[...] = own[...]

    @pl.when(w == 1)
    def _():
        put(out, product(pair(piece), pair(window)))


def stack(upper, lower):
    return tuple(jnp.concatenate([a, b], axis=0) for a, b in zip(upper, lower, strict=True))


def half(x, near, across):
    near, across = pair(near), pair(across)
    return stack(pick(x == 0, near, across), pick(x == 0, across, near))


def whole(near, across, far, far_across):
    x, k, _ = place()
    mine, theirs = half(x, near, across), half(x, far, far_across)
    return stack(pick(k == 0, mine, theirs), pick(k == 0, theirs, mine))


def before_kernel(u, block, turned, near, far, out, high, low):
    x, k, _ = place()
    one = identity(block.shape[-1])
    other = pick(k == 0, (near[...], far[...]), (far[...], near[...]))
    before = product(pick(x == 1, other, one), pick(k == 1, pair(turned), one))
    for slot, left in enumerate((pair(u[0, 0, 0]), pair(block))):
        value = product(left, before, NT)
        put(out.at[slot], value)
        for plane in range(2):
            high[slot, plane], low[slot, plane] = halves(value[plane])


def left_half(before, near, across, core, high, low):
    x, _, w = place()
    width = before[0].shape[-1] // 2

    @pl.when(w == 3)
    def _():
        strips = halves(jnp.concatenate(half(x, near, across), axis=0))
        for slot in range(2):
            value = columns_of(*before, slot, strips)
            for plane in range(2):
                high[slot, plane], low[slot, plane] = halves(value[plane])

    @pl.when((w == 1) | (w == 2))
    def _():
        at = pl.ds(pl.multiple_of(core * width, width), width)
        high[...], low[...] = (part[:, :, :, at] for part in before)


def left_kernel(before_high, before_low, near, across, high, low):
    _, k, _ = place()
    left_half((before_high, before_low), near, across, k, high, low)


def merge_kernel(one, two, three, out):
    _, _, w = place()
    out[...] = jnp.where(w == 1, one[...], jnp.where(w == 2, two[...], three[...]))


def columns_of(high, low, slot, offset):
    width = offset[0].shape[0] // 2
    dot = functools.partial(lax.dot_general, dimension_numbers=NT, preferred_element_type=F32)
    parts = []
    for plane in range(2):
        a, al = high[slot, plane], low[slot, plane]
        parts.append(dot(a, offset[0]) + (dot(a, offset[1]) + dot(al, offset[0])))
    real, imag = parts
    return real[:, :width] - imag[:, width:], real[:, width:] + imag[:, :width]


def joined(k, mine, theirs):
    def plane(slot, index):
        a, b = mine[slot, index], theirs[slot, index]
        return jnp.concatenate([jnp.where(k == 0, a, b), jnp.where(k == 0, b, a)], axis=1)

    return {(slot, index): plane(slot, index) for slot in range(2) for index in range(2)}


def near_kernel(
    before_high, before_low, far_own, far_past, high, low, early, late, out, whole_high, whole_low, far_high, far_low
):
    x, k, w = place()
    left_half((before_high, before_low), far_own, far_past, 1 - k, far_high, far_low)

    @pl.when(w != 0)
    def _():
        both_high, both_low = joined(k, high, far_high), joined(k, low, far_low)
        for slot in range(2):
            for plane in range(2):
                whole_high[slot, plane], whole_low[slot, plane] = both_high[slot, plane], both_low[slot, plane]
        offset = halves(jnp.concatenate(half(jnp.where(w == 3, 1 - x, x), early, late), axis=0))
        for slot in range(2):
            put(out.at[slot], columns_of(both_high, both_low, slot, offset))


def far_kernel(before, near, high, low, early, late, out, far, sems):
    x, k, w = place()
    width = near.shape[-1]

    @pl.when(w == 0)
    def _():
        copies = [pltpu.make_async_copy(before.at[s], out.at[0, 0, s], sems.at[s, 0]) for s in range(2)]
        for copy in copies:
            copy.start()
        for copy in copies:
            copy.wait()

    @pl.when(w != 0)
    def _():
        def start(columns, slot, core, which):
            at = pl.ds(pl.multiple_of(core * width, width), width)
            copy = pltpu.make_async_copy(columns.at[slot], out.at[0, 0, slot, :, :, at], sems.at[slot, which])
            copy.start()
            return copy

        copies = [start(near, slot, k, 0) for slot in range(2)]
        offset = halves(jnp.concatenate(half(jnp.where(w == 3, 1 - x, x), early, late), axis=0))
        for slot in range(2):
            put(far.at[slot], columns_of(high, low, slot, offset))
            copies.append(start(far, slot, 1 - k, 1))
        for copy in copies:
            copy.wait()


def permute(value, pairs):
    windows = lax.axis_size("win")
    flat = [(a * windows + b, c * windows + d) for (a, b), (c, d) in pairs]
    return lax.ppermute(value, AXES, flat)


def small(unitaries):
    width = unitaries.shape[-1]
    full, strip = (2, width, width), (2, width // 4, width)
    spots = [(t, v) for t in range(4) for v in range(4)]
    cores = [((t, v), (t ^ 1, v)) for t, v in spots]
    chips = [((t, v), (t ^ 2, v)) for t, v in spots]
    twins = [((t, v), (t, v ^ 1)) for t, v in spots]
    one_two = [((t, 1), (t, 2)) for t in range(4)]
    zero_one = [((t, 0), (t, 1)) for t in range(4)]
    two_three = [((t, 2), (t, 3)) for t in range(4)]
    onward = [((t, v), (t, (v + 1) % 4)) for t, v in spots]
    one_three = [((t, 1), (t, 3)) for t in range(4)]
    tie = lax.optimization_barrier

    block, turned = call(block_kernel, [full, full], unitaries, name="block")
    turned_other = permute(turned, cores)
    (plane,) = call(plane_kernel, [full[1:]], turned, turned_other, name="plane")
    near_chip = permute(plane, chips)
    (chip,) = call(chip_kernel, [full], turned, turned_other, plane, name="chip")
    near_chip, chip = tie((near_chip, chip))
    far_chip = permute(near_chip, cores)
    own, other = call(
        strips_kernel, [strip, strip], chip, near_chip, far_chip, name="strips", scratch=[pltpu.VMEM(full, F32)]
    )
    one = permute(own, twins)
    (window,) = call(window_kernel, [full], chip, near_chip, far_chip, name="window")
    one_other = permute(other, zero_one)
    (both,) = call(extend_kernel, [strip], one, window, other, name="extend")
    two = permute(both, onward)
    (both_other,) = call(extend_kernel, [strip], one_other, window, other, name="extend_other")
    three_other = permute(both_other, one_three)
    three = permute(two, two_three)
    two_other = permute(both_other, one_two)
    own, past = tie((one, two))
    far_own, far_past = permute(own, cores), permute(past, cores)
    far_chip, _ = tie((far_chip, two))
    both = jax.ShapeDtypeStruct((2, *full), jnp.bfloat16)
    operands = unitaries, block, turned_other, near_chip, far_chip
    before, *before_parts = call(before_kernel, [(2, *full), both, both], *operands, name="before")
    three_other, before = tie((three_other, before))
    parts = [jax.ShapeDtypeStruct((2, 2, width, width // 2), jnp.bfloat16)] * 2
    high, low = call(left_kernel, parts, *before_parts, own, past, name="left")
    three_other, high = tie((three_other, high))
    (early,) = call(merge_kernel, [strip], one, two, three_other, name="merge_early")
    far_early = permute(early, cores)
    two_other, early = tie((two_other, early))
    (other,) = call(merge_kernel, [strip], one_other, two_other, two_other, name="merge_other")
    three, other = tie((three, other))
    (late,) = call(merge_kernel, [strip], other, other, three, name="merge_late")
    far_late = permute(late, cores)
    half_width = (2, 2, width, width // 2)
    operands = *before_parts, far_own, far_past, high, low, early, late
    scratch = [pltpu.VMEM(half_width, jnp.bfloat16)] * 2
    near, high, low = call(near_kernel, [half_width, both, both], *operands, name="near", scratch=scratch)
    scratch = pltpu.VMEM(half_width, F32), pltpu.SemaphoreType.DMA((2, 2))
    operands = before, near, high, low, far_early, far_late
    (out,) = call(far_kernel, [unitaries.shape], *operands, name="far", scratch=scratch, hbm_out=True)
    return out


def multiply(left, right):
    def body(a, b, out):
        put(out, product(pair(a), pair(b)))

    return call(body, [right.shape], left, right, name="multiply")[0]


def scan(value, axis):
    count, mine = lax.axis_size(axis), lax.axis_index(axis)
    width = value.shape[-1]
    one = jnp.stack([jnp.eye(width, dtype=F32), jnp.zeros((width, width), F32)])
    shifted = lax.ppermute(value, axis, [(i, i + 1) for i in range(count - 1)])
    running = jnp.where(mine >= 1, shifted, one)
    step = 1
    while step < count - 1:
        arrived = lax.ppermute(running, axis, [(i, i + step) for i in range(count - step)])
        running = multiply(running, jnp.where(mine >= step, arrived, one))
        step *= 2
    return running


def general(unitaries):
    own = unitaries[0, 0]
    count = lax.axis_size("tm")
    block = multiply(own[1], own[0])
    before = scan(block, "tm")
    through = multiply(block, before)
    step, mine = 1, lax.axis_index("tm")
    total = through
    while step < count:
        pairs = [(count - 1 - i, count - 1 - i - step) for i in range(min(step, count - step))]
        arrived = lax.ppermute(total, "tm", pairs)
        behind = count - 1 - mine
        total = jnp.where((behind >= step) & (behind < 2 * step), arrived, total)
        step *= 2
    offset = multiply(before, scan(total, "win"))
    first = multiply(own[0], offset)
    return jnp.stack([first, multiply(own[1], first)])[None, None]


def solution(mesh):
    spec = P(("groups", "win"), "tm", None, None, None, None)
    plain = mesh.shape["tm"] == 4 and mesh.shape["win"] == 4
    return jax.shard_map(
        small if plain else general,
        mesh=mesh,
        in_specs=(spec,),
        out_specs=spec,
        check_vma=False,
    )
```

```python
import functools

import jax
import jax.numpy as jnp
from jax import lax
from jax.experimental import pallas as pl
from jax.experimental.pallas import tpu as pltpu
from jax.sharding import PartitionSpec as P

F32 = jnp.float32
AXES = ("tm", "win")
NN = (((1,), (0,)), ((), ()))
NT = (((1,), (1,)), ((), ()))


def halves(x):
    high = x.astype(jnp.bfloat16)
    return high, (x - high.astype(F32)).astype(jnp.bfloat16)


def product(left, right, dims=NN):
    (lr, lrl), (li, lil) = halves(left[0]), halves(left[1])
    (rr, rrl), (ri, ril) = halves(right[0]), halves(right[1])
    dot = functools.partial(
        lax.dot_general, dimension_numbers=dims, preferred_element_type=F32
    )

    def real(a, al, b, bl):
        return dot(a, b) + (dot(a, bl) + dot(al, b))

    return (
        real(lr, lrl, rr, rrl) - real(li, lil, ri, ril),
        real(lr, lrl, ri, ril) + real(li, lil, rr, rrl),
    )


def real_product(left, right):
    (a, al), (b, bl) = halves(left), halves(right)
    dot = functools.partial(jnp.dot, preferred_element_type=F32)
    return dot(a, b) + (dot(a, bl) + dot(al, b))


def pick(condition, yes, no):
    return tuple(jnp.where(condition, a, b) for a, b in zip(yes, no, strict=True))


def pair(ref):
    return ref[0], ref[1]


def put(ref, value):
    ref[0] = value[0]
    ref[1] = value[1]


def identity(width):
    rows = lax.broadcasted_iota(jnp.int32, (width, width), 0)
    columns = lax.broadcasted_iota(jnp.int32, (width, width), 1)
    one = (rows == columns).astype(F32)
    return one, jnp.zeros_like(one)


def call(body, outs, *operands, name, scratch=(), hbm_out=False, alias=None):
    whole, far = pl.BlockSpec(memory_space=pltpu.VMEM), pl.BlockSpec(memory_space=pl.ANY)
    shapes = [out if isinstance(out, jax.ShapeDtypeStruct) else jax.ShapeDtypeStruct(out, F32) for out in outs]
    return pl.pallas_call(
        body,
        out_shape=shapes,
        in_specs=[far if i == alias else whole for i in range(len(operands))],
        out_specs=[far if hbm_out and i == 0 else whole for i in range(len(outs))],
        input_output_aliases={} if alias is None else {alias: 0},
        scratch_shapes=list(scratch),
        compiler_params=pltpu.CompilerParams(vmem_limit_bytes=32 << 20),
        name=name,
    )(*operands)


def place():
    t, w = lax.axis_index("tm"), lax.axis_index("win")
    return t // 2, t % 2, w


def block_kernel(u, block, turned):
    b = product(pair(u[0, 0, 1]), pair(u[0, 0, 0]))
    put(block, b)
    put(turned, (b[0].T, b[1].T))


def plane_kernel(mine, theirs, plane):
    _, k, _ = place()

    @pl.when(k == 0)
    def _():
        (lr, li), (rr, ri) = pair(mine), pair(theirs)
        plane[...] = real_product(lr, rr) - real_product(li, ri)

    @pl.when(k == 1)
    def _():
        (lr, li), (rr, ri) = pair(theirs), pair(mine)
        plane[...] = real_product(lr, ri) + real_product(li, rr)


def chip_kernel(mine, theirs, plane, chip):
    _, k, _ = place()

    @pl.when(k == 0)
    def _():
        (lr, li), (rr, ri) = pair(mine), pair(theirs)
        put(chip, (plane[...], real_product(lr, ri) + real_product(li, rr)))

    @pl.when(k == 1)
    def _():
        (lr, li), (rr, ri) = pair(theirs), pair(mine)
        put(chip, (real_product(lr, rr) - real_product(li, ri), plane[...]))


def ordered(x, k, chip, near, far):
    mine = pair(chip)
    other = pick(k == 0, (near[...], far[...]), (far[...], near[...]))
    return pick(x == 0, mine, other), pick(x == 0, other, mine)


def strips_kernel(chip, near, far, own, other, scratch):
    x, k, w = place()

    @pl.when(w % 2 == 0)
    def _():
        one, two = ordered(x, k, chip, near, far)
        put(scratch, one)
        rows = own.shape[1]
        half = scratch[:, pl.ds(pl.multiple_of(2 * k * rows, 2 * rows), 2 * rows), :]
        value = product((half[0], half[1]), two)
        top, low = tuple(v[:rows] for v in value), tuple(v[rows:] for v in value)
        put(own, pick(x == 0, top, low))
        put(other, pick(x == 0, low, top))


def window_kernel(chip, near, far, window):
    x, k, w = place()

    @pl.when(w == 1)
    def _():
        put(window, product(*ordered(x, k, chip, near, far)))


def extend_kernel(piece, window, own, out):
    _, _, w = place()

    @pl.when(w == 2)
    def _():
        out[...] = own[...]

    @pl.when(w == 1)
    def _():
        put(out, product(pair(piece), pair(window)))


def stack(upper, lower):
    return tuple(jnp.concatenate([a, b], axis=0) for a, b in zip(upper, lower, strict=True))


def half(x, near, across):
    near, across = (tuple(p[...] for p in s) if isinstance(s, tuple) else pair(s) for s in (near, across))
    return stack(pick(x == 0, near, across), pick(x == 0, across, near))


def whole(near, across, far, far_across):
    x, k, _ = place()
    mine, theirs = half(x, near, across), half(x, far, far_across)
    return stack(pick(k == 0, mine, theirs), pick(k == 0, theirs, mine))


def before_kernel(u, block, turned, near, far, out, high, low):
    x, k, _ = place()
    one = identity(block.shape[-1])
    other = pick(k == 0, (near[...], far[...]), (far[...], near[...]))
    before = product(pick(x == 1, other, one), pick(k == 1, pair(turned), one))
    for slot, left in enumerate((pair(u[0, 0, 0]), pair(block))):
        value = product(left, before, NT)
        put(out.at[slot], value)
        for plane in range(2):
            high[slot, plane], low[slot, plane] = halves(value[plane])


def left_half(before, near, across, core, high, low):
    x, _, w = place()
    width = before[0].shape[-1] // 2

    @pl.when(w == 3)
    def _():
        strips = halves(jnp.concatenate(half(x, near, across), axis=0))
        for slot in range(2):
            value = columns_of(*before, slot, strips)
            for plane in range(2):
                high[slot, plane], low[slot, plane] = halves(value[plane])

    @pl.when((w == 1) | (w == 2))
    def _():
        at = pl.ds(pl.multiple_of(core * width, width), width)
        high[...], low[...] = (part[:, :, :, at] for part in before)


def left_kernel(before_high, before_low, near, across, high, low):
    _, k, _ = place()
    left_half((before_high, before_low), near, across, k, high, low)


def planes_kernel(one, two, *outs):
    rows = jnp.concatenate([one[0], one[1], two[0], two[1]], axis=0)
    start = 0
    for out in outs:
        out[...] = rows[start : start + out.shape[0]]
        start += out.shape[0]


def merge_kernel(one, two, three, out):
    _, _, w = place()
    out[...] = jnp.where(w == 1, one[...], jnp.where(w == 2, two[...], three[...]))


def columns_of(high, low, slot, offset):
    width = offset[0].shape[0] // 2
    dot = functools.partial(lax.dot_general, dimension_numbers=NT, preferred_element_type=F32)
    parts = []
    for plane in range(2):
        a, al = high[slot, plane], low[slot, plane]
        parts.append(dot(a, offset[0]) + (dot(a, offset[1]) + dot(al, offset[0])))
    real, imag = parts
    return real[:, :width] - imag[:, width:], real[:, width:] + imag[:, :width]


def joined(k, mine, theirs):
    def plane(slot, index):
        a, b = mine[slot, index], theirs[slot, index]
        return jnp.concatenate([jnp.where(k == 0, a, b), jnp.where(k == 0, b, a)], axis=1)

    return {(slot, index): plane(slot, index) for slot in range(2) for index in range(2)}


def left_far_kernel(before_high, before_low, *refs):
    _, k, _ = place()
    *pieces, high, low = refs
    rows = jnp.concatenate([piece[...] for piece in pieces], axis=0)
    a, b, c, d = (rows[i * rows.shape[0] // 4 : (i + 1) * rows.shape[0] // 4] for i in range(4))
    left_half((before_high, before_low), (a, b), (c, d), 1 - k, high, low)


def near_kernel(high, low, far_high, far_low, early, late, out, whole_high, whole_low):
    x, k, w = place()

    @pl.when(w != 0)
    def _():
        both_high, both_low = joined(k, high, far_high), joined(k, low, far_low)
        for slot in range(2):
            for plane in range(2):
                whole_high[slot, plane], whole_low[slot, plane] = both_high[slot, plane], both_low[slot, plane]
        offset = halves(jnp.concatenate(half(jnp.where(w == 3, 1 - x, x), early, late), axis=0))
        for slot in range(2):
            put(out.at[slot], columns_of(both_high, both_low, slot, offset))


def far_kernel(before, near, high, low, early, late, out, far, sems):
    x, k, w = place()
    width = near.shape[-1]

    @pl.when(w == 0)
    def _():
        copies = [pltpu.make_async_copy(before.at[s], out.at[0, 0, s], sems.at[s, 0]) for s in range(2)]
        for copy in copies:
            copy.start()
        for copy in copies:
            copy.wait()

    @pl.when(w != 0)
    def _():
        def start(columns, slot, core, which):
            at = pl.ds(pl.multiple_of(core * width, width), width)
            copy = pltpu.make_async_copy(columns.at[slot], out.at[0, 0, slot, :, :, at], sems.at[slot, which])
            copy.start()
            return copy

        copies = [start(near, slot, k, 0) for slot in range(2)]
        offset = halves(jnp.concatenate(half(jnp.where(w == 3, 1 - x, x), early, late), axis=0))
        for slot in range(2):
            put(far.at[slot], columns_of(high, low, slot, offset))
            copies.append(start(far, slot, 1 - k, 1))
        for copy in copies:
            copy.wait()


def permute(value, pairs):
    windows = lax.axis_size("win")
    flat = [(a * windows + b, c * windows + d) for (a, b), (c, d) in pairs]
    return lax.ppermute(value, AXES, flat)


def small(unitaries):
    width = unitaries.shape[-1]
    full, strip = (2, width, width), (2, width // 4, width)
    spots = [(t, v) for t in range(4) for v in range(4)]
    cores = [((t, v), (t ^ 1, v)) for t, v in spots]
    chips = [((t, v), (t ^ 2, v)) for t, v in spots]
    twins = [((t, v), (t, v ^ 1)) for t, v in spots]
    one_two = [((t, 1), (t, 2)) for t in range(4)]
    zero_one = [((t, 0), (t, 1)) for t in range(4)]
    two_three = [((t, 2), (t, 3)) for t in range(4)]
    onward = [((t, v), (t, (v + 1) % 4)) for t, v in spots]
    one_three = [((t, 1), (t, 3)) for t in range(4)]
    tie = lax.optimization_barrier

    block, turned = call(block_kernel, [full, full], unitaries, name="block")
    turned_other = permute(turned, cores)
    (plane,) = call(plane_kernel, [full[1:]], turned, turned_other, name="plane")
    near_chip = permute(plane, chips)
    (chip,) = call(chip_kernel, [full], turned, turned_other, plane, name="chip")
    near_chip, chip = tie((near_chip, chip))
    far_chip = permute(near_chip, cores)
    own, other = call(
        strips_kernel, [strip, strip], chip, near_chip, far_chip, name="strips", scratch=[pltpu.VMEM(full, F32)]
    )
    one = permute(own, twins)
    (window,) = call(window_kernel, [full], chip, near_chip, far_chip, name="window")
    one_other = permute(other, zero_one)
    (both,) = call(extend_kernel, [strip], one, window, other, name="extend")
    two = permute(both, onward)
    (both_other,) = call(extend_kernel, [strip], one_other, window, other, name="extend_other")
    three_other = permute(both_other, one_three)
    far_chip, _ = tie((far_chip, both_other))
    both = jax.ShapeDtypeStruct((2, *full), jnp.bfloat16)
    operands = unitaries, block, turned_other, near_chip, far_chip
    before, *before_parts = call(before_kernel, [(2, *full), both, both], *operands, name="before")
    two, before = tie((two, before))
    three = permute(two, two_three)
    two_other = permute(both_other, one_two)
    own, past = tie((one, two))
    thirds = [(3 * width // 8, width)] + [(5 * width // 16, width)] * 2
    planes = call(planes_kernel, thirds, own, past, name="planes")
    far_strips = [permute(plane, cores) for plane in planes]
    three_other, before = tie((three_other, before))
    parts = [jax.ShapeDtypeStruct((2, 2, width, width // 2), jnp.bfloat16)] * 2
    high, low = call(left_kernel, parts, *before_parts, own, past, name="left")
    three_other, high = tie((three_other, high))
    (early,) = call(merge_kernel, [strip], one, two, three_other, name="merge_early")
    far_early = permute(early, cores)
    two_other, early = tie((two_other, early))
    (other,) = call(merge_kernel, [strip], one_other, two_other, two_other, name="merge_other")
    far_high, far_low = call(left_far_kernel, parts, *before_parts, *far_strips, name="left_far")
    three, other, far_high = tie((three, other, far_high))
    (late,) = call(merge_kernel, [strip], other, other, three, name="merge_late")
    far_late = permute(late, cores)
    half_width = (2, 2, width, width // 2)
    operands = high, low, far_high, far_low, early, late
    near, high, low = call(near_kernel, [half_width, both, both], *operands, name="near")
    scratch = pltpu.VMEM(half_width, F32), pltpu.SemaphoreType.DMA((2, 2))
    operands = before, near, high, low, far_early, far_late
    (out,) = call(far_kernel, [unitaries.shape], *operands, name="far", scratch=scratch, hbm_out=True)
    return out


def multiply(left, right):
    def body(a, b, out):
        put(out, product(pair(a), pair(b)))

    return call(body, [right.shape], left, right, name="multiply")[0]


def scan(value, axis):
    count, mine = lax.axis_size(axis), lax.axis_index(axis)
    width = value.shape[-1]
    one = jnp.stack([jnp.eye(width, dtype=F32), jnp.zeros((width, width), F32)])
    shifted = lax.ppermute(value, axis, [(i, i + 1) for i in range(count - 1)])
    running = jnp.where(mine >= 1, shifted, one)
    step = 1
    while step < count - 1:
        arrived = lax.ppermute(running, axis, [(i, i + step) for i in range(count - step)])
        running = multiply(running, jnp.where(mine >= step, arrived, one))
        step *= 2
    return running


def general(unitaries):
    own = unitaries[0, 0]
    count = lax.axis_size("tm")
    block = multiply(own[1], own[0])
    before = scan(block, "tm")
    through = multiply(block, before)
    step, mine = 1, lax.axis_index("tm")
    total = through
    while step < count:
        pairs = [(count - 1 - i, count - 1 - i - step) for i in range(min(step, count - step))]
        arrived = lax.ppermute(total, "tm", pairs)
        behind = count - 1 - mine
        total = jnp.where((behind >= step) & (behind < 2 * step), arrived, total)
        step *= 2
    offset = multiply(before, scan(total, "win"))
    first = multiply(own[0], offset)
    return jnp.stack([first, multiply(own[1], first)])[None, None]


def solution(mesh):
    spec = P(("groups", "win"), "tm", None, None, None, None)
    plain = mesh.shape["tm"] == 4 and mesh.shape["win"] == 4
    return jax.shard_map(
        small if plain else general,
        mesh=mesh,
        in_specs=(spec,),
        out_specs=spec,
        check_vma=False,
    )
```

```python
import functools

import jax
import jax.numpy as jnp
from jax import lax
from jax.experimental import pallas as pl
from jax.experimental.pallas import tpu as pltpu
from jax.sharding import PartitionSpec as P

F32 = jnp.float32
AXES = ("tm", "win")
NN = (((1,), (0,)), ((), ()))
NT = (((1,), (1,)), ((), ()))


def halves(x):
    high = x.astype(jnp.bfloat16)
    return high, (x - high.astype(F32)).astype(jnp.bfloat16)


def product(left, right, dims=NN):
    (lr, lrl), (li, lil) = halves(left[0]), halves(left[1])
    (rr, rrl), (ri, ril) = halves(right[0]), halves(right[1])
    dot = functools.partial(
        lax.dot_general, dimension_numbers=dims, preferred_element_type=F32
    )

    def real(a, al, b, bl):
        return dot(a, b) + (dot(a, bl) + dot(al, b))

    return (
        real(lr, lrl, rr, rrl) - real(li, lil, ri, ril),
        real(lr, lrl, ri, ril) + real(li, lil, rr, rrl),
    )


def real_product(left, right):
    (a, al), (b, bl) = halves(left), halves(right)
    dot = functools.partial(jnp.dot, preferred_element_type=F32)
    return dot(a, b) + (dot(a, bl) + dot(al, b))


def pick(condition, yes, no):
    return tuple(jnp.where(condition, a, b) for a, b in zip(yes, no, strict=True))


def pair(ref):
    return ref[0], ref[1]


def put(ref, value):
    ref[0] = value[0]
    ref[1] = value[1]


def identity(width):
    rows = lax.broadcasted_iota(jnp.int32, (width, width), 0)
    columns = lax.broadcasted_iota(jnp.int32, (width, width), 1)
    one = (rows == columns).astype(F32)
    return one, jnp.zeros_like(one)


def call(body, outs, *operands, name, scratch=(), hbm_out=False, alias=None):
    whole, far = pl.BlockSpec(memory_space=pltpu.VMEM), pl.BlockSpec(memory_space=pl.ANY)
    shapes = [out if isinstance(out, jax.ShapeDtypeStruct) else jax.ShapeDtypeStruct(out, F32) for out in outs]
    return pl.pallas_call(
        body,
        out_shape=shapes,
        in_specs=[far if i == alias else whole for i in range(len(operands))],
        out_specs=[far if hbm_out and i == 0 else whole for i in range(len(outs))],
        input_output_aliases={} if alias is None else {alias: 0},
        scratch_shapes=list(scratch),
        compiler_params=pltpu.CompilerParams(vmem_limit_bytes=32 << 20),
        name=name,
    )(*operands)


def place():
    t, w = lax.axis_index("tm"), lax.axis_index("win")
    return t // 2, t % 2, w


def block_kernel(u, block, turned):
    b = product(pair(u[0, 0, 1]), pair(u[0, 0, 0]))
    put(block, b)
    put(turned, (b[0].T, b[1].T))


def plane_kernel(mine, theirs, plane):
    _, k, _ = place()

    @pl.when(k == 0)
    def _():
        (lr, li), (rr, ri) = pair(mine), pair(theirs)
        plane[...] = real_product(lr, rr) - real_product(li, ri)

    @pl.when(k == 1)
    def _():
        (lr, li), (rr, ri) = pair(theirs), pair(mine)
        plane[...] = real_product(lr, ri) + real_product(li, rr)


def chip_kernel(mine, theirs, plane, chip):
    _, k, _ = place()

    @pl.when(k == 0)
    def _():
        (lr, li), (rr, ri) = pair(mine), pair(theirs)
        put(chip, (plane[...], real_product(lr, ri) + real_product(li, rr)))

    @pl.when(k == 1)
    def _():
        (lr, li), (rr, ri) = pair(theirs), pair(mine)
        put(chip, (real_product(lr, rr) - real_product(li, ri), plane[...]))


def ordered(x, k, chip, near, far):
    mine = pair(chip)
    other = pick(k == 0, (near[...], far[...]), (far[...], near[...]))
    return pick(x == 0, mine, other), pick(x == 0, other, mine)


def strips_kernel(chip, near, far, own, other):
    x, k, w = place()
    rows = own.shape[1]
    at = pl.ds(pl.multiple_of(2 * k * rows, 2 * rows), 2 * rows)

    @pl.when((w % 2 == 0) & (x == 0))
    def _():
        half = chip[:, at, :]
        right = pick(k == 0, (near[...], far[...]), (far[...], near[...]))
        value = product((half[0], half[1]), right)
        put(own, tuple(v[:rows] for v in value))
        put(other, tuple(v[rows:] for v in value))

    @pl.when((w % 2 == 0) & (x == 1))
    def _():
        near_half, far_half = near[at, :], far[at, :]
        left = pick(k == 0, (near_half, far_half), (far_half, near_half))
        value = product(left, pair(chip))
        put(own, tuple(v[rows:] for v in value))
        put(other, tuple(v[:rows] for v in value))


def window_kernel(chip, near, far, window):
    x, k, w = place()

    @pl.when(w == 1)
    def _():
        put(window, product(*ordered(x, k, chip, near, far)))


def extend_kernel(piece, window, own, out):
    _, _, w = place()

    @pl.when(w == 2)
    def _():
        out[...] = own[...]

    @pl.when(w == 1)
    def _():
        put(out, product(pair(piece), pair(window)))


def stack(upper, lower):
    return tuple(jnp.concatenate([a, b], axis=0) for a, b in zip(upper, lower, strict=True))


def half(x, near, across):
    near, across = (tuple(p[...] for p in s) if isinstance(s, tuple) else pair(s) for s in (near, across))
    return stack(pick(x == 0, near, across), pick(x == 0, across, near))


def whole(near, across, far, far_across):
    x, k, _ = place()
    mine, theirs = half(x, near, across), half(x, far, far_across)
    return stack(pick(k == 0, mine, theirs), pick(k == 0, theirs, mine))


def before_kernel(u, block, turned, near, far, out, high, low):
    x, k, _ = place()
    one = identity(block.shape[-1])
    other = pick(k == 0, (near[...], far[...]), (far[...], near[...]))
    before = product(pick(x == 1, other, one), pick(k == 1, pair(turned), one))
    for slot, left in enumerate((pair(u[0, 0, 0]), pair(block))):
        value = product(left, before, NT)
        put(out.at[slot], value)
        for plane in range(2):
            high[slot, plane], low[slot, plane] = halves(value[plane])


def left_half(before, near, across, core, high, low):
    x, _, w = place()
    width = before[0].shape[-1] // 2

    @pl.when(w == 3)
    def _():
        strips = halves(jnp.concatenate(half(x, near, across), axis=0))
        for slot in range(2):
            value = columns_of(*before, slot, strips)
            for plane in range(2):
                high[slot, plane], low[slot, plane] = halves(value[plane])

    @pl.when((w == 1) | (w == 2))
    def _():
        at = pl.ds(pl.multiple_of(core * width, width), width)
        high[...], low[...] = (part[:, :, :, at] for part in before)


def left_kernel(before_high, before_low, near, across, high, low):
    _, k, _ = place()
    left_half((before_high, before_low), near, across, k, high, low)


def planes_kernel(one, two, *outs):
    rows = jnp.concatenate([one[0], one[1], two[0], two[1]], axis=0)
    start = 0
    for out in outs:
        out[...] = rows[start : start + out.shape[0]]
        start += out.shape[0]


def merge_kernel(one, two, three, out):
    _, _, w = place()
    out[...] = jnp.where(w == 1, one[...], jnp.where(w == 2, two[...], three[...]))


def columns_of(high, low, slot, offset):
    width = offset[0].shape[0] // 2
    dot = functools.partial(lax.dot_general, dimension_numbers=NT, preferred_element_type=F32)
    parts = []
    for plane in range(2):
        a, al = high[slot, plane], low[slot, plane]
        parts.append(dot(a, offset[0]) + (dot(a, offset[1]) + dot(al, offset[0])))
    real, imag = parts
    return real[:, :width] - imag[:, width:], real[:, width:] + imag[:, :width]


def joined(k, mine, theirs):
    def plane(slot, index):
        a, b = mine[slot, index], theirs[slot, index]
        return jnp.concatenate([jnp.where(k == 0, a, b), jnp.where(k == 0, b, a)], axis=1)

    return {(slot, index): plane(slot, index) for slot in range(2) for index in range(2)}


def left_far_kernel(before_high, before_low, *refs):
    _, k, _ = place()
    *pieces, high, low = refs
    rows = jnp.concatenate([piece[...] for piece in pieces], axis=0)
    a, b, c, d = (rows[i * rows.shape[0] // 4 : (i + 1) * rows.shape[0] // 4] for i in range(4))
    left_half((before_high, before_low), (a, b), (c, d), 1 - k, high, low)


def near_kernel(high, low, far_high, far_low, early, late, out, whole_high, whole_low):
    x, k, w = place()

    @pl.when(w != 0)
    def _():
        both_high, both_low = joined(k, high, far_high), joined(k, low, far_low)
        for slot in range(2):
            for plane in range(2):
                whole_high[slot, plane], whole_low[slot, plane] = both_high[slot, plane], both_low[slot, plane]
        offset = halves(jnp.concatenate(half(jnp.where(w == 3, 1 - x, x), early, late), axis=0))
        for slot in range(2):
            put(out.at[slot], columns_of(both_high, both_low, slot, offset))


def far_kernel(before, near, high, low, early, late, out, far, sems):
    x, k, w = place()
    width = near.shape[-1]

    @pl.when(w == 0)
    def _():
        copies = [pltpu.make_async_copy(before.at[s], out.at[0, 0, s], sems.at[s, 0]) for s in range(2)]
        for copy in copies:
            copy.start()
        for copy in copies:
            copy.wait()

    @pl.when(w != 0)
    def _():
        def start(columns, slot, core, which):
            at = pl.ds(pl.multiple_of(core * width, width), width)
            copy = pltpu.make_async_copy(columns.at[slot], out.at[0, 0, slot, :, :, at], sems.at[slot, which])
            copy.start()
            return copy

        copies = [start(near, slot, k, 0) for slot in range(2)]
        offset = halves(jnp.concatenate(half(jnp.where(w == 3, 1 - x, x), early, late), axis=0))
        for slot in range(2):
            put(far.at[slot], columns_of(high, low, slot, offset))
            copies.append(start(far, slot, 1 - k, 1))
        for copy in copies:
            copy.wait()


def permute(value, pairs):
    windows = lax.axis_size("win")
    flat = [(a * windows + b, c * windows + d) for (a, b), (c, d) in pairs]
    return lax.ppermute(value, AXES, flat)


def small(unitaries):
    width = unitaries.shape[-1]
    full, strip = (2, width, width), (2, width // 4, width)
    spots = [(t, v) for t in range(4) for v in range(4)]
    cores = [((t, v), (t ^ 1, v)) for t, v in spots]
    chips = [((t, v), (t ^ 2, v)) for t, v in spots]
    twins = [((t, v), (t, v ^ 1)) for t, v in spots]
    one_two = [((t, 1), (t, 2)) for t in range(4)]
    zero_one = [((t, 0), (t, 1)) for t in range(4)]
    two_three = [((t, 2), (t, 3)) for t in range(4)]
    onward = [((t, v), (t, (v + 1) % 4)) for t, v in spots]
    one_three = [((t, 1), (t, 3)) for t in range(4)]
    tie = lax.optimization_barrier

    block, turned = call(block_kernel, [full, full], unitaries, name="block")
    turned_other = permute(turned, cores)
    (plane,) = call(plane_kernel, [full[1:]], turned, turned_other, name="plane")
    near_chip = permute(plane, chips)
    (chip,) = call(chip_kernel, [full], turned, turned_other, plane, name="chip")
    near_chip, chip = tie((near_chip, chip))
    far_chip = permute(near_chip, cores)
    own, other = call(strips_kernel, [strip, strip], chip, near_chip, far_chip, name="strips")
    one = permute(own, twins)
    (window,) = call(window_kernel, [full], chip, near_chip, far_chip, name="window")
    one_other = permute(other, zero_one)
    (both,) = call(extend_kernel, [strip], one, window, other, name="extend")
    two = permute(both, onward)
    (both_other,) = call(extend_kernel, [strip], one_other, window, other, name="extend_other")
    three_other = permute(both_other, one_three)
    far_chip, _ = tie((far_chip, both_other))
    both = jax.ShapeDtypeStruct((2, *full), jnp.bfloat16)
    operands = unitaries, block, turned_other, near_chip, far_chip
    before, *before_parts = call(before_kernel, [(2, *full), both, both], *operands, name="before")
    two, before = tie((two, before))
    three = permute(two, two_three)
    two_other = permute(both_other, one_two)
    own, past = tie((one, two))
    thirds = [(3 * width // 8, width)] + [(5 * width // 16, width)] * 2
    planes = call(planes_kernel, thirds, own, past, name="planes")
    far_strips = [permute(plane, cores) for plane in planes]
    three_other, before = tie((three_other, before))
    parts = [jax.ShapeDtypeStruct((2, 2, width, width // 2), jnp.bfloat16)] * 2
    high, low = call(left_kernel, parts, *before_parts, own, past, name="left")
    three_other, high = tie((three_other, high))
    (early,) = call(merge_kernel, [strip], one, two, three_other, name="merge_early")
    far_early = permute(early, cores)
    two_other, early = tie((two_other, early))
    (other,) = call(merge_kernel, [strip], one_other, two_other, two_other, name="merge_other")
    far_high, far_low = call(left_far_kernel, parts, *before_parts, *far_strips, name="left_far")
    three, other, far_high = tie((three, other, far_high))
    (late,) = call(merge_kernel, [strip], other, other, three, name="merge_late")
    far_late = permute(late, cores)
    half_width = (2, 2, width, width // 2)
    operands = high, low, far_high, far_low, early, late
    near, high, low = call(near_kernel, [half_width, both, both], *operands, name="near")
    scratch = pltpu.VMEM(half_width, F32), pltpu.SemaphoreType.DMA((2, 2))
    operands = before, near, high, low, far_early, far_late
    (out,) = call(far_kernel, [unitaries.shape], *operands, name="far", scratch=scratch, hbm_out=True)
    return out


def multiply(left, right):
    def body(a, b, out):
        put(out, product(pair(a), pair(b)))

    return call(body, [right.shape], left, right, name="multiply")[0]


def scan(value, axis):
    count, mine = lax.axis_size(axis), lax.axis_index(axis)
    width = value.shape[-1]
    one = jnp.stack([jnp.eye(width, dtype=F32), jnp.zeros((width, width), F32)])
    shifted = lax.ppermute(value, axis, [(i, i + 1) for i in range(count - 1)])
    running = jnp.where(mine >= 1, shifted, one)
    step = 1
    while step < count - 1:
        arrived = lax.ppermute(running, axis, [(i, i + step) for i in range(count - step)])
        running = multiply(running, jnp.where(mine >= step, arrived, one))
        step *= 2
    return running


def general(unitaries):
    own = unitaries[0, 0]
    count = lax.axis_size("tm")
    block = multiply(own[1], own[0])
    before = scan(block, "tm")
    through = multiply(block, before)
    step, mine = 1, lax.axis_index("tm")
    total = through
    while step < count:
        pairs = [(count - 1 - i, count - 1 - i - step) for i in range(min(step, count - step))]
        arrived = lax.ppermute(total, "tm", pairs)
        behind = count - 1 - mine
        total = jnp.where((behind >= step) & (behind < 2 * step), arrived, total)
        step *= 2
    offset = multiply(before, scan(total, "win"))
    first = multiply(own[0], offset)
    return jnp.stack([first, multiply(own[1], first)])[None, None]


def solution(mesh):
    spec = P(("groups", "win"), "tm", None, None, None, None)
    plain = mesh.shape["tm"] == 4 and mesh.shape["win"] == 4
    return jax.shard_map(
        small if plain else general,
        mesh=mesh,
        in_specs=(spec,),
        out_specs=spec,
        check_vma=False,
    )
```

```python
import functools

import jax
import jax.numpy as jnp
from jax import lax
from jax.experimental import pallas as pl
from jax.experimental.pallas import tpu as pltpu
from jax.sharding import PartitionSpec as P

F32 = jnp.float32
AXES = ("tm", "win")
NN = (((1,), (0,)), ((), ()))
NT = (((1,), (1,)), ((), ()))


def halves(x):
    high = x.astype(jnp.bfloat16)
    return high, (x - high.astype(F32)).astype(jnp.bfloat16)


def product(left, right, dims=NN):
    (lr, lrl), (li, lil) = halves(left[0]), halves(left[1])
    (rr, rrl), (ri, ril) = halves(right[0]), halves(right[1])
    dot = functools.partial(
        lax.dot_general, dimension_numbers=dims, preferred_element_type=F32
    )

    def real(a, al, b, bl):
        return dot(a, b) + (dot(a, bl) + dot(al, b))

    return (
        real(lr, lrl, rr, rrl) - real(li, lil, ri, ril),
        real(lr, lrl, ri, ril) + real(li, lil, rr, rrl),
    )


def real_product(left, right):
    (a, al), (b, bl) = halves(left), halves(right)
    dot = functools.partial(jnp.dot, preferred_element_type=F32)
    return dot(a, b) + (dot(a, bl) + dot(al, b))


def pick(condition, yes, no):
    return tuple(jnp.where(condition, a, b) for a, b in zip(yes, no, strict=True))


def pair(ref):
    return ref[0], ref[1]


def put(ref, value):
    ref[0] = value[0]
    ref[1] = value[1]


def identity(width):
    rows = lax.broadcasted_iota(jnp.int32, (width, width), 0)
    columns = lax.broadcasted_iota(jnp.int32, (width, width), 1)
    one = (rows == columns).astype(F32)
    return one, jnp.zeros_like(one)


def call(body, outs, *operands, name, scratch=(), hbm_out=False, alias=None):
    whole, far = pl.BlockSpec(memory_space=pltpu.VMEM), pl.BlockSpec(memory_space=pl.ANY)
    shapes = [out if isinstance(out, jax.ShapeDtypeStruct) else jax.ShapeDtypeStruct(out, F32) for out in outs]
    return pl.pallas_call(
        body,
        out_shape=shapes,
        in_specs=[far if i == alias else whole for i in range(len(operands))],
        out_specs=[far if hbm_out and i == 0 else whole for i in range(len(outs))],
        input_output_aliases={} if alias is None else {alias: 0},
        scratch_shapes=list(scratch),
        compiler_params=pltpu.CompilerParams(vmem_limit_bytes=32 << 20),
        name=name,
    )(*operands)


def place():
    t, w = lax.axis_index("tm"), lax.axis_index("win")
    return t // 2, t % 2, w


def block_kernel(u, block, turned):
    b = product(pair(u[0, 0, 1]), pair(u[0, 0, 0]))
    put(block, b)
    put(turned, (b[0].T, b[1].T))


def plane_kernel(mine, theirs, plane):
    _, k, _ = place()

    @pl.when(k == 0)
    def _():
        (lr, li), (rr, ri) = pair(mine), pair(theirs)
        plane[...] = real_product(lr, rr) - real_product(li, ri)

    @pl.when(k == 1)
    def _():
        (lr, li), (rr, ri) = pair(theirs), pair(mine)
        plane[...] = real_product(lr, ri) + real_product(li, rr)


def chip_kernel(mine, theirs, plane, chip):
    _, k, _ = place()

    @pl.when(k == 0)
    def _():
        (lr, li), (rr, ri) = pair(mine), pair(theirs)
        put(chip, (plane[...], real_product(lr, ri) + real_product(li, rr)))

    @pl.when(k == 1)
    def _():
        (lr, li), (rr, ri) = pair(theirs), pair(mine)
        put(chip, (real_product(lr, rr) - real_product(li, ri), plane[...]))


def ordered(x, k, chip, near, far):
    mine = pair(chip)
    other = pick(k == 0, (near[...], far[...]), (far[...], near[...]))
    return pick(x == 0, mine, other), pick(x == 0, other, mine)


def strips_kernel(chip, near, far, own, other):
    x, k, w = place()
    rows = own.shape[1]
    at = pl.ds(pl.multiple_of(2 * k * rows, 2 * rows), 2 * rows)

    @pl.when((w % 2 == 0) & (x == 0))
    def _():
        half = chip[:, at, :]
        right = pick(k == 0, (near[...], far[...]), (far[...], near[...]))
        value = product((half[0], half[1]), right)
        put(own, tuple(v[:rows] for v in value))
        put(other, tuple(v[rows:] for v in value))

    @pl.when((w % 2 == 0) & (x == 1))
    def _():
        near_half, far_half = near[at, :], far[at, :]
        left = pick(k == 0, (near_half, far_half), (far_half, near_half))
        value = product(left, pair(chip))
        put(own, tuple(v[rows:] for v in value))
        put(other, tuple(v[:rows] for v in value))


def window_kernel(chip, near, far, window):
    x, k, w = place()

    @pl.when(w == 1)
    def _():
        put(window, product(*ordered(x, k, chip, near, far)))


def extend_kernel(piece, window, own, out):
    _, _, w = place()

    @pl.when(w == 2)
    def _():
        out[...] = own[...]

    @pl.when(w == 1)
    def _():
        put(out, product(pair(piece), pair(window)))


def stack(upper, lower):
    return tuple(jnp.concatenate([a, b], axis=0) for a, b in zip(upper, lower, strict=True))


def half(x, near, across):
    near, across = (tuple(p[...] for p in s) if isinstance(s, tuple) else pair(s) for s in (near, across))
    return stack(pick(x == 0, near, across), pick(x == 0, across, near))


def whole(near, across, far, far_across):
    x, k, _ = place()
    mine, theirs = half(x, near, across), half(x, far, far_across)
    return stack(pick(k == 0, mine, theirs), pick(k == 0, theirs, mine))


def before_kernel(u, block, turned, near, far, out, high, low):
    x, k, _ = place()
    one = identity(block.shape[-1])
    other = pick(k == 0, (near[...], far[...]), (far[...], near[...]))
    before = product(pick(x == 1, other, one), pick(k == 1, pair(turned), one))
    for slot, left in enumerate((pair(u[0, 0, 0]), pair(block))):
        value = product(left, before, NT)
        put(out.at[slot], value)
        for plane in range(2):
            high[slot, plane], low[slot, plane] = halves(value[plane])


def left_half(before, near, across, core, high, low):
    x, _, w = place()
    width = before[0].shape[-1] // 2

    @pl.when(w == 3)
    def _():
        strips = halves(jnp.concatenate(half(x, near, across), axis=0))
        for slot in range(2):
            value = columns_of(*before, slot, strips)
            for plane in range(2):
                high[slot, plane], low[slot, plane] = halves(value[plane])

    @pl.when((w == 1) | (w == 2))
    def _():
        at = pl.ds(pl.multiple_of(core * width, width), width)
        high[...], low[...] = (part[:, :, :, at] for part in before)


def left_kernel(before_high, before_low, near, across, high, low):
    _, k, _ = place()
    left_half((before_high, before_low), near, across, k, high, low)


def planes_kernel(one, two, *outs):
    rows = jnp.concatenate([one[0], one[1], two[0], two[1]], axis=0)
    start = 0
    for out in outs:
        out[...] = rows[start : start + out.shape[0]]
        start += out.shape[0]


def merge_kernel(one, two, three, out):
    _, _, w = place()
    out[...] = jnp.where(w == 1, one[...], jnp.where(w == 2, two[...], three[...]))


def columns_of(high, low, slot, offset):
    width = offset[0].shape[0] // 2
    dot = functools.partial(lax.dot_general, dimension_numbers=NT, preferred_element_type=F32)
    parts = []
    for plane in range(2):
        a, al = high[slot, plane], low[slot, plane]
        parts.append(dot(a, offset[0]) + (dot(a, offset[1]) + dot(al, offset[0])))
    real, imag = parts
    return real[:, :width] - imag[:, width:], real[:, width:] + imag[:, :width]


def left_far_kernel(before_high, before_low, *refs):
    _, k, _ = place()
    *pieces, high, low = refs
    rows = jnp.concatenate([piece[...] for piece in pieces], axis=0)
    a, b, c, d = (rows[i * rows.shape[0] // 4 : (i + 1) * rows.shape[0] // 4] for i in range(4))
    left_half((before_high, before_low), (a, b), (c, d), 1 - k, high, low)


def near_kernel(high, low, far_high, far_low, early, late, out, whole_high, whole_low):
    x, k, w = place()
    width = high.shape[-1]

    @pl.when(w != 0)
    def _():
        for core, parts in ((k, (high, low)), (1 - k, (far_high, far_low))):
            at = pl.ds(pl.multiple_of(core * width, width), width)
            for part, joined in zip(parts, (whole_high, whole_low), strict=True):
                joined[:, :, :, at] = part[...]
        offset = halves(jnp.concatenate(half(jnp.where(w == 3, 1 - x, x), early, late), axis=0))
        for slot in range(2):
            put(out.at[slot], columns_of(whole_high, whole_low, slot, offset))


def far_kernel(before, near, high, low, early, late, out, far, sems):
    x, k, w = place()
    width = near.shape[-1]

    @pl.when(w == 0)
    def _():
        copies = [pltpu.make_async_copy(before.at[s], out.at[0, 0, s], sems.at[s, 0]) for s in range(2)]
        for copy in copies:
            copy.start()
        for copy in copies:
            copy.wait()

    @pl.when(w != 0)
    def _():
        def start(columns, slot, core, which):
            at = pl.ds(pl.multiple_of(core * width, width), width)
            copy = pltpu.make_async_copy(columns.at[slot], out.at[0, 0, slot, :, :, at], sems.at[slot, which])
            copy.start()
            return copy

        copies = [start(near, slot, k, 0) for slot in range(2)]
        offset = halves(jnp.concatenate(half(jnp.where(w == 3, 1 - x, x), early, late), axis=0))
        for slot in range(2):
            put(far.at[slot], columns_of(high, low, slot, offset))
            copies.append(start(far, slot, 1 - k, 1))
        for copy in copies:
            copy.wait()


def permute(value, pairs):
    windows = lax.axis_size("win")
    flat = [(a * windows + b, c * windows + d) for (a, b), (c, d) in pairs]
    return lax.ppermute(value, AXES, flat)


def small(unitaries):
    width = unitaries.shape[-1]
    full, strip = (2, width, width), (2, width // 4, width)
    spots = [(t, v) for t in range(4) for v in range(4)]
    cores = [((t, v), (t ^ 1, v)) for t, v in spots]
    chips = [((t, v), (t ^ 2, v)) for t, v in spots]
    twins = [((t, v), (t, v ^ 1)) for t, v in spots]
    one_two = [((t, 1), (t, 2)) for t in range(4)]
    zero_one = [((t, 0), (t, 1)) for t in range(4)]
    two_three = [((t, 2), (t, 3)) for t in range(4)]
    onward = [((t, v), (t, (v + 1) % 4)) for t, v in spots]
    one_three = [((t, 1), (t, 3)) for t in range(4)]
    tie = lax.optimization_barrier

    block, turned = call(block_kernel, [full, full], unitaries, name="block")
    turned_other = permute(turned, cores)
    (plane,) = call(plane_kernel, [full[1:]], turned, turned_other, name="plane")
    near_chip = permute(plane, chips)
    (chip,) = call(chip_kernel, [full], turned, turned_other, plane, name="chip")
    near_chip, chip = tie((near_chip, chip))
    far_chip = permute(near_chip, cores)
    own, other = call(strips_kernel, [strip, strip], chip, near_chip, far_chip, name="strips")
    one = permute(own, twins)
    (window,) = call(window_kernel, [full], chip, near_chip, far_chip, name="window")
    one_other = permute(other, zero_one)
    (both,) = call(extend_kernel, [strip], one, window, other, name="extend")
    two = permute(both, onward)
    (both_other,) = call(extend_kernel, [strip], one_other, window, other, name="extend_other")
    three_other = permute(both_other, one_three)
    far_chip, _ = tie((far_chip, both_other))
    both = jax.ShapeDtypeStruct((2, *full), jnp.bfloat16)
    operands = unitaries, block, turned_other, near_chip, far_chip
    before, *before_parts = call(before_kernel, [(2, *full), both, both], *operands, name="before")
    two, before = tie((two, before))
    three = permute(two, two_three)
    two_other = permute(both_other, one_two)
    own, past = tie((one, two))
    thirds = [(3 * width // 8, width)] + [(5 * width // 16, width)] * 2
    planes = call(planes_kernel, thirds, own, past, name="planes")
    far_strips = [permute(plane, cores) for plane in planes]
    parts = [jax.ShapeDtypeStruct((2, 2, width, width // 2), jnp.bfloat16)] * 2
    high, low = call(left_kernel, parts, *before_parts, own, past, name="left")
    three_other, high = tie((three_other, high))
    (early,) = call(merge_kernel, [strip], one, two, three_other, name="merge_early")
    far_early = permute(early, cores)
    two_other, early = tie((two_other, early))
    (other,) = call(merge_kernel, [strip], one_other, two_other, two_other, name="merge_other")
    far_high, far_low = call(left_far_kernel, parts, *before_parts, *far_strips, name="left_far")
    three, other, far_high = tie((three, other, far_high))
    (late,) = call(merge_kernel, [strip], other, other, three, name="merge_late")
    far_late = permute(late, cores)
    half_width = (2, 2, width, width // 2)
    operands = high, low, far_high, far_low, early, late
    near, high, low = call(near_kernel, [half_width, both, both], *operands, name="near")
    scratch = pltpu.VMEM(half_width, F32), pltpu.SemaphoreType.DMA((2, 2))
    operands = before, near, high, low, far_early, far_late
    (out,) = call(far_kernel, [unitaries.shape], *operands, name="far", scratch=scratch, hbm_out=True)
    return out


def multiply(left, right):
    def body(a, b, out):
        put(out, product(pair(a), pair(b)))

    return call(body, [right.shape], left, right, name="multiply")[0]


def scan(value, axis):
    count, mine = lax.axis_size(axis), lax.axis_index(axis)
    width = value.shape[-1]
    one = jnp.stack([jnp.eye(width, dtype=F32), jnp.zeros((width, width), F32)])
    shifted = lax.ppermute(value, axis, [(i, i + 1) for i in range(count - 1)])
    running = jnp.where(mine >= 1, shifted, one)
    step = 1
    while step < count - 1:
        arrived = lax.ppermute(running, axis, [(i, i + step) for i in range(count - step)])
        running = multiply(running, jnp.where(mine >= step, arrived, one))
        step *= 2
    return running


def general(unitaries):
    own = unitaries[0, 0]
    count = lax.axis_size("tm")
    block = multiply(own[1], own[0])
    before = scan(block, "tm")
    through = multiply(block, before)
    step, mine = 1, lax.axis_index("tm")
    total = through
    while step < count:
        pairs = [(count - 1 - i, count - 1 - i - step) for i in range(min(step, count - step))]
        arrived = lax.ppermute(total, "tm", pairs)
        behind = count - 1 - mine
        total = jnp.where((behind >= step) & (behind < 2 * step), arrived, total)
        step *= 2
    offset = multiply(before, scan(total, "win"))
    first = multiply(own[0], offset)
    return jnp.stack([first, multiply(own[1], first)])[None, None]


def solution(mesh):
    spec = P(("groups", "win"), "tm", None, None, None, None)
    plain = mesh.shape["tm"] == 4 and mesh.shape["win"] == 4
    return jax.shard_map(
        small if plain else general,
        mesh=mesh,
        in_specs=(spec,),
        out_specs=spec,
        check_vma=False,
    )
```

```python
import functools

import jax
import jax.numpy as jnp
from jax import lax
from jax.experimental import pallas as pl
from jax.experimental.pallas import tpu as pltpu
from jax.sharding import PartitionSpec as P

F32 = jnp.float32
AXES = ("tm", "win")
NN = (((1,), (0,)), ((), ()))
NT = (((1,), (1,)), ((), ()))


def halves(x):
    high = x.astype(jnp.bfloat16)
    return high, (x - high.astype(F32)).astype(jnp.bfloat16)


def product(left, right, dims=NN):
    (lr, lrl), (li, lil) = halves(left[0]), halves(left[1])
    (rr, rrl), (ri, ril) = halves(right[0]), halves(right[1])
    dot = functools.partial(
        lax.dot_general, dimension_numbers=dims, preferred_element_type=F32
    )

    def real(a, al, b, bl):
        return dot(a, b) + (dot(a, bl) + dot(al, b))

    return (
        real(lr, lrl, rr, rrl) - real(li, lil, ri, ril),
        real(lr, lrl, ri, ril) + real(li, lil, rr, rrl),
    )


def real_product(left, right):
    (a, al), (b, bl) = halves(left), halves(right)
    dot = functools.partial(jnp.dot, preferred_element_type=F32)
    return dot(a, b) + (dot(a, bl) + dot(al, b))


def pick(condition, yes, no):
    return tuple(jnp.where(condition, a, b) for a, b in zip(yes, no, strict=True))


def pair(ref):
    return ref[0], ref[1]


def put(ref, value):
    ref[0] = value[0]
    ref[1] = value[1]


def identity(width):
    rows = lax.broadcasted_iota(jnp.int32, (width, width), 0)
    columns = lax.broadcasted_iota(jnp.int32, (width, width), 1)
    one = (rows == columns).astype(F32)
    return one, jnp.zeros_like(one)


def call(body, outs, *operands, name, scratch=(), hbm_out=False, alias=None):
    whole, far = pl.BlockSpec(memory_space=pltpu.VMEM), pl.BlockSpec(memory_space=pl.ANY)
    shapes = [out if isinstance(out, jax.ShapeDtypeStruct) else jax.ShapeDtypeStruct(out, F32) for out in outs]
    return pl.pallas_call(
        body,
        out_shape=shapes,
        in_specs=[far if i == alias else whole for i in range(len(operands))],
        out_specs=[far if hbm_out and i == 0 else whole for i in range(len(outs))],
        input_output_aliases={} if alias is None else {alias: 0},
        scratch_shapes=list(scratch),
        compiler_params=pltpu.CompilerParams(vmem_limit_bytes=32 << 20),
        name=name,
    )(*operands)


def place():
    t, w = lax.axis_index("tm"), lax.axis_index("win")
    return t // 2, t % 2, w


def block_kernel(u, block, turned):
    b = product(pair(u[0, 0, 1]), pair(u[0, 0, 0]))
    put(block, b)
    put(turned, (b[0].T, b[1].T))


def plane_kernel(mine, theirs, plane):
    _, k, _ = place()

    @pl.when(k == 0)
    def _():
        (lr, li), (rr, ri) = pair(mine), pair(theirs)
        plane[...] = real_product(lr, rr) - real_product(li, ri)

    @pl.when(k == 1)
    def _():
        (lr, li), (rr, ri) = pair(theirs), pair(mine)
        plane[...] = real_product(lr, ri) + real_product(li, rr)


def chip_kernel(mine, theirs, plane, chip):
    _, k, _ = place()

    @pl.when(k == 0)
    def _():
        (lr, li), (rr, ri) = pair(mine), pair(theirs)
        put(chip, (plane[...], real_product(lr, ri) + real_product(li, rr)))

    @pl.when(k == 1)
    def _():
        (lr, li), (rr, ri) = pair(theirs), pair(mine)
        put(chip, (real_product(lr, rr) - real_product(li, ri), plane[...]))


def ordered(x, k, chip, near, far):
    mine = pair(chip)
    other = pick(k == 0, (near[...], far[...]), (far[...], near[...]))
    return pick(x == 0, mine, other), pick(x == 0, other, mine)


def strips_kernel(chip, near, far, own, other):
    x, k, w = place()
    rows = own.shape[1]
    at = pl.ds(pl.multiple_of(2 * k * rows, 2 * rows), 2 * rows)

    @pl.when((w % 2 == 0) & (x == 0))
    def _():
        half = chip[:, at, :]
        right = pick(k == 0, (near[...], far[...]), (far[...], near[...]))
        value = product((half[0], half[1]), right)
        put(own, tuple(v[:rows] for v in value))
        put(other, tuple(v[rows:] for v in value))

    @pl.when((w % 2 == 0) & (x == 1))
    def _():
        near_half, far_half = near[at, :], far[at, :]
        left = pick(k == 0, (near_half, far_half), (far_half, near_half))
        value = product(left, pair(chip))
        put(own, tuple(v[rows:] for v in value))
        put(other, tuple(v[:rows] for v in value))


def window_kernel(chip, near, far, window):
    x, k, w = place()

    @pl.when(w == 1)
    def _():
        put(window, product(*ordered(x, k, chip, near, far)))


def extend_kernel(piece, window, own, out):
    _, _, w = place()

    @pl.when(w == 2)
    def _():
        out[...] = own[...]

    @pl.when(w == 1)
    def _():
        put(out, product(pair(piece), pair(window)))


def stack(upper, lower):
    return tuple(jnp.concatenate([a, b], axis=0) for a, b in zip(upper, lower, strict=True))


def half(x, near, across):
    near, across = (tuple(p[...] for p in s) if isinstance(s, tuple) else pair(s) for s in (near, across))
    return stack(pick(x == 0, near, across), pick(x == 0, across, near))


def whole(near, across, far, far_across):
    x, k, _ = place()
    mine, theirs = half(x, near, across), half(x, far, far_across)
    return stack(pick(k == 0, mine, theirs), pick(k == 0, theirs, mine))


def before_kernel(u, block, turned, near, far, out, high, low):
    x, k, _ = place()
    one = identity(block.shape[-1])
    other = pick(k == 0, (near[...], far[...]), (far[...], near[...]))
    before = product(pick(x == 1, other, one), pick(k == 1, pair(turned), one))
    for slot, left in enumerate((pair(u[0, 0, 0]), pair(block))):
        value = product(left, before, NT)
        put(out.at[slot], value)
        for plane in range(2):
            high[slot, plane], low[slot, plane] = halves(value[plane])


def left_half(before, near, across, core, high, low):
    x, _, w = place()
    width = before[0].shape[-1] // 2

    @pl.when(w == 3)
    def _():
        strips = halves(jnp.concatenate(half(x, near, across), axis=0))
        for slot in range(2):
            value = columns_of(*before, slot, strips)
            for plane in range(2):
                high[slot, plane], low[slot, plane] = halves(value[plane])

    @pl.when((w == 1) | (w == 2))
    def _():
        at = pl.ds(pl.multiple_of(core * width, width), width)
        high[...], low[...] = (part[:, :, :, at] for part in before)


def left_kernel(before_high, before_low, near, across, high, low):
    _, k, _ = place()
    left_half((before_high, before_low), near, across, k, high, low)


def planes_kernel(one, two, *outs):
    rows = jnp.concatenate([one[0], one[1], two[0], two[1]], axis=0)
    start = 0
    for out in outs:
        out[...] = rows[start : start + out.shape[0]]
        start += out.shape[0]


def merge_kernel(one, two, three, out):
    _, _, w = place()
    out[...] = jnp.where(w == 1, one[...], jnp.where(w == 2, two[...], three[...]))


def columns_of(high, low, slot, offset):
    width = offset[0].shape[0] // 2
    dot = functools.partial(lax.dot_general, dimension_numbers=NT, preferred_element_type=F32)
    parts = []
    for plane in range(2):
        a, al = high[slot, plane], low[slot, plane]
        parts.append(dot(a, offset[0]) + (dot(a, offset[1]) + dot(al, offset[0])))
    real, imag = parts
    return real[:, :width] - imag[:, width:], real[:, width:] + imag[:, :width]


def left_far_kernel(before_high, before_low, *refs):
    _, k, _ = place()
    *pieces, high, low = refs
    rows = jnp.concatenate([piece[...] for piece in pieces], axis=0)
    a, b, c, d = (rows[i * rows.shape[0] // 4 : (i + 1) * rows.shape[0] // 4] for i in range(4))
    left_half((before_high, before_low), (a, b), (c, d), 1 - k, high, low)


def near_kernel(high, low, far_high, far_low, early, late, out, whole_high, whole_low):
    x, k, w = place()
    width = high.shape[-1]

    @pl.when(w != 0)
    def _():
        for core, parts in ((k, (high, low)), (1 - k, (far_high, far_low))):
            at = pl.ds(pl.multiple_of(core * width, width), width)
            for part, joined in zip(parts, (whole_high, whole_low), strict=True):
                joined[:, :, :, at] = part[...]
        offset = halves(jnp.concatenate(half(jnp.where(w == 3, 1 - x, x), early, late), axis=0))
        for slot in range(2):
            put(out.at[slot], columns_of(whole_high, whole_low, slot, offset))


def far_kernel(before, near, high, low, early, late, out, far, sems):
    x, k, w = place()
    width = near.shape[-1]

    @pl.when(w == 0)
    def _():
        copies = [pltpu.make_async_copy(before.at[s], out.at[0, 0, s], sems.at[s, 0]) for s in range(2)]
        for copy in copies:
            copy.start()
        for copy in copies:
            copy.wait()

    @pl.when(w != 0)
    def _():
        def start(columns, slot, core, which):
            at = pl.ds(pl.multiple_of(core * width, width), width)
            copy = pltpu.make_async_copy(columns.at[slot], out.at[0, 0, slot, :, :, at], sems.at[slot, which])
            copy.start()
            return copy

        copies = [start(near, slot, k, 0) for slot in range(2)]
        offset = halves(jnp.concatenate(half(jnp.where(w == 3, 1 - x, x), early, late), axis=0))
        for slot in range(2):
            put(far.at[slot], columns_of(high, low, slot, offset))
            copies.append(start(far, slot, 1 - k, 1))
        for copy in copies:
            copy.wait()


def permute(value, pairs):
    windows = lax.axis_size("win")
    flat = [(a * windows + b, c * windows + d) for (a, b), (c, d) in pairs]
    return lax.ppermute(value, AXES, flat)


def small(unitaries):
    width = unitaries.shape[-1]
    full, strip = (2, width, width), (2, width // 4, width)
    spots = [(t, v) for t in range(4) for v in range(4)]
    cores = [((t, v), (t ^ 1, v)) for t, v in spots]
    chips = [((t, v), (t ^ 2, v)) for t, v in spots]
    twins = [((t, v), (t, v ^ 1)) for t, v in spots]
    one_two = [((t, 1), (t, 2)) for t in range(4)]
    zero_one = [((t, 0), (t, 1)) for t in range(4)]
    two_three = [((t, 2), (t, 3)) for t in range(4)]
    onward = [((t, v), (t, (v + 1) % 4)) for t, v in spots]
    one_three = [((t, 1), (t, 3)) for t in range(4)]
    tie = lax.optimization_barrier

    block, turned = call(block_kernel, [full, full], unitaries, name="block")
    turned_other = permute(turned, cores)
    (plane,) = call(plane_kernel, [full[1:]], turned, turned_other, name="plane")
    near_chip = permute(plane, chips)
    (chip,) = call(chip_kernel, [full], turned, turned_other, plane, name="chip")
    near_chip, chip = tie((near_chip, chip))
    far_chip = permute(near_chip, cores)
    own, other = call(strips_kernel, [strip, strip], chip, near_chip, far_chip, name="strips")
    one = permute(own, twins)
    (window,) = call(window_kernel, [full], chip, near_chip, far_chip, name="window")
    one_other = permute(other, zero_one)
    (both,) = call(extend_kernel, [strip], one, window, other, name="extend")
    two = permute(both, onward)
    (both_other,) = call(extend_kernel, [strip], one_other, window, other, name="extend_other")
    three_other = permute(both_other, one_three)
    far_chip, _ = tie((far_chip, both_other))
    both = jax.ShapeDtypeStruct((2, *full), jnp.bfloat16)
    operands = unitaries, block, turned_other, near_chip, far_chip
    before, *before_parts = call(before_kernel, [(2, *full), both, both], *operands, name="before")
    two, before = tie((two, before))
    three = permute(two, two_three)
    two_other = permute(both_other, one_two)
    own, past = tie((one, two))
    thirds = [(3 * width // 8, width)] + [(5 * width // 16, width)] * 2
    planes = call(planes_kernel, thirds, own, past, name="planes")
    far_strips = [permute(plane, cores) for plane in planes]
    parts = [jax.ShapeDtypeStruct((2, 2, width, width // 2), jnp.bfloat16)] * 2
    high, low = call(left_kernel, parts, *before_parts, own, past, name="left")
    three_other, high = tie((three_other, high))
    (early,) = call(merge_kernel, [strip], one, two, three_other, name="merge_early")
    far_early = permute(early, cores)
    (other,) = call(merge_kernel, [strip], one_other, two_other, two_other, name="merge_other")
    far_high, far_low = call(left_far_kernel, parts, *before_parts, *far_strips, name="left_far")
    three, other, far_high = tie((three, other, far_high))
    (late,) = call(merge_kernel, [strip], other, other, three, name="merge_late")
    far_late = permute(late, cores)
    half_width = (2, 2, width, width // 2)
    operands = high, low, far_high, far_low, early, late
    near, high, low = call(near_kernel, [half_width, both, both], *operands, name="near")
    scratch = pltpu.VMEM(half_width, F32), pltpu.SemaphoreType.DMA((2, 2))
    operands = before, near, high, low, far_early, far_late
    (out,) = call(far_kernel, [unitaries.shape], *operands, name="far", scratch=scratch, hbm_out=True)
    return out


def multiply(left, right):
    def body(a, b, out):
        put(out, product(pair(a), pair(b)))

    return call(body, [right.shape], left, right, name="multiply")[0]


def scan(value, axis):
    count, mine = lax.axis_size(axis), lax.axis_index(axis)
    width = value.shape[-1]
    one = jnp.stack([jnp.eye(width, dtype=F32), jnp.zeros((width, width), F32)])
    shifted = lax.ppermute(value, axis, [(i, i + 1) for i in range(count - 1)])
    running = jnp.where(mine >= 1, shifted, one)
    step = 1
    while step < count - 1:
        arrived = lax.ppermute(running, axis, [(i, i + step) for i in range(count - step)])
        running = multiply(running, jnp.where(mine >= step, arrived, one))
        step *= 2
    return running


def general(unitaries):
    own = unitaries[0, 0]
    count = lax.axis_size("tm")
    block = multiply(own[1], own[0])
    before = scan(block, "tm")
    through = multiply(block, before)
    step, mine = 1, lax.axis_index("tm")
    total = through
    while step < count:
        pairs = [(count - 1 - i, count - 1 - i - step) for i in range(min(step, count - step))]
        arrived = lax.ppermute(total, "tm", pairs)
        behind = count - 1 - mine
        total = jnp.where((behind >= step) & (behind < 2 * step), arrived, total)
        step *= 2
    offset = multiply(before, scan(total, "win"))
    first = multiply(own[0], offset)
    return jnp.stack([first, multiply(own[1], first)])[None, None]


def solution(mesh):
    spec = P(("groups", "win"), "tm", None, None, None, None)
    plain = mesh.shape["tm"] == 4 and mesh.shape["win"] == 4
    return jax.shard_map(
        small if plain else general,
        mesh=mesh,
        in_specs=(spec,),
        out_specs=spec,
        check_vma=False,
    )
```
